32 devices in a mesh: section: 4 (over y, x), expert: 8 (over z, core).
Axes of the slice: x: 2, y: 2, z: 4, core: 2. Of those that a mesh axis runs over, the one named last changes fastest.
Arguments:
- inputs: bfloat16 [2, 512, 2048], P(None, 'expert'), may hold values from -45 to 45
- cotangent: bfloat16 [2, 512, 2048], P(None, 'expert'), may hold values from -6 to 6
- lengths: int32 [2, 8], P(None, 'expert'), may hold values from 32 to 64, as said below
- norm_gain: float32 [4, 2048], P('section'), may hold values from 0.1 to 1.9
- router: bfloat16 [4, 2048, 8], P('section'), may hold values from -0.125 to 0.125
- expert_in: bfloat16 [4, 8, 2048, 1536], P('section', 'expert'), may hold values from -0.125 to 0.125
- expert_out: bfloat16 [4, 8, 768, 2048], P('section', 'expert'), may hold values from -0.21875 to 0.21875
- routes: int32 [4, 2, 512, 2], P('section', None, 'expert'), may hold values from 0 to 7, as said below
Outputs:
- section_grads: bfloat16 [4, 2, 512, 2048], P('section', None, 'expert')
- router_grad: float32 [4, 2048, 8], P('section')
- gain_grad: float32 [4, 2048], P('section')
The draws below stay inside these ranges and needn't reach their ends.
Inputs may be any that keep to these rules, and one draw needn't show every extreme that they name: `lengths`: sequence b of a micro-batch fills positions b * 64 to b * 64 + length - 1; the rest is padding. Each micro-batch has a sequence of length 64. `routes`: each row names 2 different experts. Among the rows of one sequence for one section and micro-batch no expert is named more than 16 times; for each section and micro-batch one expert is named exactly 16 times within the first 32 rows of every sequence. For each section and micro-batch the experts fall into two halves, a row's first choice in one and its second in the other.
All inputs are finite; a program needn't handle non-finite values.
Results may differ from the reference program's by a relative error of at most 0.024.
Values may be sent and summed in bfloat16 or wider, within the bound.
No kernel may reach another device: no remote copies, remote signals or barrier semaphores. Data moves between devices by JAX's collectives and lax.ppermute only.
A program may use at most 128 MiB of HBM per device.

```python
import math
import jax
import jax.numpy as jnp
from jax import lax

D = 2048
F = 768
TOPK = 2
MICRO = 2
TOK_DEV = 64
EXPERTS = 8
SECTIONS = 4
SEQS = 8
TOKENS = 512
CAP = 16
N_EXPERT = 8


def draw_inputs(key, part):
    key_rows, key_cols, key_vals = jax.random.split(key, 3)
    row_scale = jnp.exp(jax.random.uniform(key_rows, (MICRO, TOKENS, 1), jnp.float32, math.log(0.3), math.log(3.0)))
    col_scale = jnp.exp(jax.random.uniform(key_cols, (1, 1, D), jnp.float32, math.log(0.3), math.log(3.0)))
    base_values = jnp.clip(jax.random.normal(key_vals, (MICRO, TOKENS, D), jnp.float32), -5.0, 5.0)
    return (base_values * row_scale * col_scale).astype(jnp.bfloat16)


def draw_lengths(key, part):
    key_len, key_full = jax.random.split(key)
    drawn_lengths = jax.random.randint(key_len, (MICRO, SEQS), TOK_DEV // 2, TOK_DEV + 1)
    full_at = jax.random.randint(key_full, (MICRO, 1), 0, SEQS)
    sequence_ids = jnp.arange(SEQS, dtype=jnp.int32)[None, :]
    return jnp.where(sequence_ids == full_at, TOK_DEV, drawn_lengths).astype(jnp.int32)


def route_block(block_key, group_first, group_second):
    key_hot, key_rest, key_second = jax.random.split(block_key, 3)
    rest_count = (EXPERTS // 2 - 1) * CAP
    hot_rows = jax.random.permutation(key_hot, TOK_DEV // 2)[:CAP]
    hot_mask = jnp.zeros((TOK_DEV,), jnp.int32).at[hot_rows].set(1)
    rest_order = jax.random.permutation(key_rest, rest_count)
    rest_rank = jnp.clip(jnp.cumsum(1 - hot_mask) - 1, 0, rest_count - 1)
    first_pick = jnp.where(hot_mask > 0, group_first[0], group_first[1 + rest_order[rest_rank] // CAP])
    second_order = jax.random.permutation(key_second, EXPERTS // 2 * CAP)
    second_pick = group_second[second_order[:TOK_DEV] // CAP]
    return jnp.stack([first_pick, second_pick], axis=1)


def draw_routes(key, part):
    group_keys = jax.random.split(jax.random.fold_in(key, 11), SECTIONS * MICRO)

    def draw_group(group_key):
        key_perm, key_blocks = jax.random.split(group_key)
        expert_order = jax.random.permutation(key_perm, EXPERTS)
        group_first = expert_order[:EXPERTS // 2]
        group_second = expert_order[EXPERTS // 2:]
        block_keys = jax.random.split(key_blocks, SEQS)

        def one_block(block_key):
            return route_block(block_key, group_first, group_second)
        return jax.vmap(one_block)(block_keys).reshape(TOKENS, 2)
    return jax.vmap(draw_group)(group_keys).reshape(SECTIONS, MICRO, TOKENS, 2).astype(jnp.int32)


def level_of(key, extent, cuts, smallest, top_value):
    level, own = 1.0, jax.random.fold_in(key, 6)
    for dim, shards_of in cuts:
        steps = jnp.exp(jax.random.uniform(jax.random.fold_in(own, dim), (shards_of,), jnp.float32, smallest / len(cuts), top_value / len(cuts)))
        level = level * jnp.repeat(steps, extent[dim] // shards_of).reshape([-1 if axis == dim else 1 for axis in range(len(extent))])
    return level


def noise(rng, shape, scale, most, cuts=(), kind=jnp.bfloat16):
    entries = jax.random.normal(rng, shape, jnp.float32) * scale
    if len(cuts) > 0:
        entries = level_of(rng, shape, cuts, -0.22, 0.18) * entries
    return jnp.clip(entries, min=-most, max=most).astype(kind)


def setup_inputs(seed: int = 0) -> dict:
    streams_of = jax.random.split(jax.random.key(seed), 9)
    inputs = draw_inputs(jax.random.fold_in(streams_of[8], 71), 0)
    cotangent = noise(streams_of[1], (MICRO, TOKENS, D), 1.0, 6.0, ((1, 8),))
    lengths = draw_lengths(jax.random.fold_in(streams_of[8], 71), 0)
    norm_gain = jnp.clip(1.0 + 0.18 * jax.random.normal(streams_of[3], (SECTIONS, D), jnp.float32), 0.1, 1.9)
    router = noise(streams_of[4], (SECTIONS, D, EXPERTS), D ** -0.5, 0.125, ((0, 4),))
    expert_in = noise(streams_of[5], (SECTIONS, EXPERTS, D, 2 * F), D ** -0.5, 0.125, ((0, 4), (1, 8)))
    expert_out = noise(streams_of[6], (SECTIONS, EXPERTS, F, D), F ** -0.5, 0.21875, ((0, 4), (1, 8)))
    routes = draw_routes(jax.random.fold_in(streams_of[8], 71), 0)
    return {"inputs": inputs, "cotangent": cotangent, "lengths": lengths, "norm_gain": norm_gain, "router": router, "expert_in": expert_in, "expert_out": expert_out, "routes": routes}


EPSILON = 1e-06

def normalize(hidden_in, gain_row):
    values = hidden_in.astype(jnp.float32)
    scale_inv = lax.rsqrt(lax.optimization_barrier(jnp.mean(values * values, axis=-1, keepdims=True)) + EPSILON)
    normed = (values * scale_inv * gain_row).astype(jnp.bfloat16)
    return (values, scale_inv, normed)

def expert_mix(row_block, weight_in):
    return jnp.dot(row_block, weight_in, preferred_element_type=jnp.float32)

def expert_apply(row_block, weight_in, weight_out):
    hidden = weight_out.shape[0]
    mixed_rows = expert_mix(row_block, weight_in)
    gate_part = mixed_rows[:, :hidden]
    up_part = mixed_rows[:, hidden:]
    activated = (gate_part * jax.nn.sigmoid(gate_part) * up_part).astype(jnp.bfloat16)
    return jnp.dot(activated, weight_out, preferred_element_type=jnp.float32).astype(jnp.bfloat16)

def expert_adjoint(mixed_rows, grad_rows, weight_in, weight_out):
    hidden = weight_out.shape[0]
    gate_part = mixed_rows[:, :hidden]
    up_part = mixed_rows[:, hidden:]
    act_grad = jnp.dot(grad_rows, weight_out.T, preferred_element_type=jnp.float32)
    sigmoid_gate = jax.nn.sigmoid(gate_part)
    gate_grad = act_grad * up_part * sigmoid_gate * (1.0 + gate_part * (1.0 - sigmoid_gate))
    up_grad = act_grad * gate_part * sigmoid_gate
    joined = jnp.concatenate([gate_grad, up_grad], axis=1).astype(jnp.bfloat16)
    return jnp.dot(joined, weight_in.T, preferred_element_type=jnp.float32).astype(jnp.bfloat16)

def route_weights(normed, router_section, route_rows):
    logits = jnp.dot(normed, router_section, preferred_element_type=jnp.float32)
    picked = jnp.take_along_axis(logits, route_rows, axis=1)
    return jax.nn.sigmoid(picked - picked[:, ::-1])

def expert_rows_of(pair_experts, pair_live, expert_id, most_rows):
    selected = (pair_experts == expert_id) & pair_live
    indices = jnp.nonzero(selected, size=most_rows, fill_value=0)[0].astype(jnp.int32)
    valid_rows = jnp.arange(most_rows) < jnp.sum(selected.astype(jnp.int32))
    return (indices, valid_rows)

def reference(inputs, cotangent, lengths, norm_gain, router, expert_in, expert_out, routes):
    most_rows = N_EXPERT * CAP
    pair_count = TOKENS * TOPK
    seq_of = jnp.arange(TOKENS) // TOK_DEV
    pos_in = jnp.arange(TOKENS) % TOK_DEV
    live_all = pos_in[None, :] < lengths[:, seq_of]
    expert_ids = jnp.arange(EXPERTS, dtype=jnp.int32)
    current = [inputs[micro_pos] for micro_pos in range(MICRO)]
    saved_inputs = []
    saved_pairs = []
    for section_pos in range(SECTIONS):
        gain_row = norm_gain[section_pos]
        router_section = router[section_pos]
        weight_in_all = expert_in[section_pos]
        weight_out_all = expert_out[section_pos]
        section_in = []
        section_pairs = []
        for micro_pos in range(MICRO):
            hidden_in = current[micro_pos]
            route_rows = routes[section_pos, micro_pos]
            pair_experts = route_rows.reshape(-1)
            pair_live = jnp.repeat(live_all[micro_pos], TOPK)

            def forward_layer(hidden_arg):
                values, scale_inv, normed = normalize(hidden_arg, gain_row)
                weights = route_weights(normed, router_section, route_rows)

                def one_expert(packed):
                    weight_in, weight_out, expert_id = packed
                    indices, valid_rows = expert_rows_of(pair_experts, pair_live, expert_id, most_rows)
                    result = expert_apply(normed[indices // TOPK], weight_in, weight_out)
                    return (indices, jnp.where(valid_rows[:, None], result, jnp.zeros_like(result)))
                indices, results = lax.map(one_expert, (weight_in_all, weight_out_all, expert_ids))
                pair_rows = jnp.zeros((pair_count, D), jnp.bfloat16).at[indices.reshape(-1)].add(results.reshape(-1, D))
                per_choice = pair_rows.reshape(TOKENS, TOPK, D).astype(jnp.float32)
                combined = lax.optimization_barrier(jnp.sum(weights[:, :, None] * per_choice, axis=1))
                return ((values + combined).astype(jnp.bfloat16), pair_rows)
            updated, pair_rows = forward_layer(hidden_in)
            section_in.append(hidden_in)
            section_pairs.append(pair_rows)
            current[micro_pos] = updated
        saved_inputs.append(section_in)
        saved_pairs.append(section_pairs)
    denominator = MICRO * TOPK * TOK_DEV
    grads_next = [cotangent[micro_pos] for micro_pos in range(MICRO)]
    section_list = [None] * SECTIONS
    router_list = [None] * SECTIONS
    gain_list = [None] * SECTIONS
    for section_pos in reversed(range(SECTIONS)):
        gain_row = norm_gain[section_pos]
        router_section = router[section_pos]
        weight_in_all = expert_in[section_pos]
        weight_out_all = expert_out[section_pos]
        router_sum = jnp.zeros((D, EXPERTS), jnp.float32)
        gain_sum = jnp.zeros((D,), jnp.float32)
        section_rows = []
        for micro_pos in range(MICRO):
            route_rows = routes[section_pos, micro_pos]
            pair_experts = route_rows.reshape(-1)
            pair_live = jnp.repeat(live_all[micro_pos], TOPK)

            def backward_layer(packed):
                hidden_arg, pair_rows, grad_arg = packed
                grad_values = grad_arg.astype(jnp.float32)
                values, scale_inv, normed = normalize(hidden_arg, gain_row)
                weights = route_weights(normed, router_section, route_rows)
                per_choice = pair_rows.reshape(TOKENS, TOPK, D).astype(jnp.float32)
                choice_grad = lax.optimization_barrier(jnp.sum(grad_values[:, None, :] * per_choice, axis=-1))
                first_grad = weights[:, 0] * weights[:, 1] * (choice_grad[:, 0] - choice_grad[:, 1])
                pick_grad = jnp.stack([first_grad, -first_grad], axis=1)
                chosen = route_rows[:, :, None] == expert_ids[None, None, :]
                logit_grad = lax.optimization_barrier(jnp.sum(jnp.where(chosen, pick_grad[:, :, None], 0.0), axis=1)).astype(jnp.bfloat16)
                output_grad = (weights[:, :, None] * grad_values[:, None, :]).astype(jnp.bfloat16).reshape(pair_count, D)

                def one_expert(packed_expert):
                    weight_in, weight_out, expert_id = packed_expert
                    indices, valid_rows = expert_rows_of(pair_experts, pair_live, expert_id, most_rows)
                    mixed_rows = expert_mix(normed[indices // TOPK], weight_in)
                    result = expert_adjoint(mixed_rows, output_grad[indices], weight_in, weight_out)
                    return (indices, jnp.where(valid_rows[:, None], result, jnp.zeros_like(result)))
                indices, results = lax.map(one_expert, (weight_in_all, weight_out_all, expert_ids))
                back_rows = jnp.zeros((pair_count, D), jnp.bfloat16).at[indices.reshape(-1)].add(results.reshape(-1, D))
                normed_grad = lax.optimization_barrier(jnp.sum(back_rows.reshape(TOKENS, TOPK, D).astype(jnp.float32), axis=1))
                normed_grad = normed_grad + jnp.dot(logit_grad, router_section.T, preferred_element_type=jnp.float32)
                centred = values * scale_inv
                scaled_grad = normed_grad * gain_row
                input_grad = grad_values + scale_inv * (scaled_grad - centred * lax.optimization_barrier(jnp.mean(scaled_grad * centred, axis=-1, keepdims=True)))
                router_piece = lax.dot_general(normed, logit_grad, (((0,), (0,)), ((), ())), preferred_element_type=jnp.float32)
                return (input_grad.astype(jnp.bfloat16), router_piece, lax.optimization_barrier(jnp.sum(normed_grad * centred, axis=0)))
            operands = (saved_inputs[section_pos][micro_pos], saved_pairs[section_pos][micro_pos], grads_next[micro_pos])
            input_grad, router_piece, gain_piece = backward_layer(operands)
            router_sum = router_sum + router_piece
            gain_sum = gain_sum + gain_piece
            section_rows.append(input_grad)
            grads_next[micro_pos] = input_grad
        section_list[section_pos] = jnp.stack(section_rows, axis=0)
        router_list[section_pos] = router_sum / denominator
        gain_list[section_pos] = gain_sum / denominator
    return (jnp.stack(section_list, axis=0), jnp.stack(router_list, axis=0), jnp.stack(gain_list, axis=0))
```

```python
import jax
import jax.numpy as jnp
from jax import lax
from jax.sharding import PartitionSpec as P

EPSILON = 1e-06
EXTRA = 128
F32 = jnp.float32
BF16 = jnp.bfloat16


def normalize(hidden_in, gain_row):
    values = hidden_in.astype(F32)
    scale_inv = lax.rsqrt(jnp.mean(values * values, axis=-1, keepdims=True) + EPSILON)
    normed = (values * scale_inv * gain_row).astype(BF16)
    return (values, scale_inv, normed)


def dot(a, b):
    return jnp.dot(a, b, preferred_element_type=F32)


def dot_t(a, b):
    return lax.dot_general(a, b, (((1,), (1,)), ((), ())), preferred_element_type=F32)


def activate(mixed):
    hidden = mixed.shape[1] // 2
    gate, up = (mixed[:, :hidden], mixed[:, hidden:])
    return (gate * jax.nn.sigmoid(gate) * up).astype(BF16)


def adjoint(mixed, grad_rows, weight_in, weight_out):
    hidden = mixed.shape[1] // 2
    gate, up = (mixed[:, :hidden], mixed[:, hidden:])
    act_grad = dot_t(grad_rows, weight_out)
    s = jax.nn.sigmoid(gate)
    gate_grad = act_grad * up * s * (1.0 + gate * (1.0 - s))
    up_grad = act_grad * gate * s
    joined = jnp.concatenate([gate_grad, up_grad], axis=1).astype(BF16)
    choice_grad = jnp.sum(act_grad * (gate * s * up), axis=1, keepdims=True)
    return (dot_t(joined, weight_in).astype(BF16), choice_grad)


def split_pair(column):
    high = column.astype(BF16)
    low = (column - high.astype(F32)).astype(BF16)
    pad = jnp.zeros((column.shape[0], EXTRA - 2), BF16)
    return jnp.concatenate([high, low, pad], axis=1)


def use_permutes(count):
    return count <= 8 and count & (count - 1) == 0


def exchange(rows, count):
    if not use_permutes(count):
        shape = (count, rows.shape[0] // count, rows.shape[1])
        return lax.all_to_all(rows.reshape(shape), "expert", 0, 0, tiled=True).reshape(rows.shape)
    size = rows.shape[0] // count
    got = [None] * count
    got[0] = rows[:size]
    for x in sorted(range(1, count), reverse=True):
        block = rows[x * size : (x + 1) * size]
        got[x] = lax.ppermute(block, "expert", [(i, i ^ x) for i in range(count)])
    return jnp.concatenate(got, axis=0)


def pair_tables(routes, live, experts, capacity, my_index):
    micros, tokens, choices = routes.shape
    codes = lax.broadcasted_iota(jnp.int32, (1, 1, 1, experts), 3)
    chosen = routes[..., None] == codes
    marked = (chosen & live[:, :, None, None]).reshape(micros, tokens * choices, experts)
    marked = marked.astype(jnp.int32)
    earlier = jnp.cumsum(marked, axis=1) - marked
    position = jnp.sum(earlier * marked, axis=2)
    present = jnp.sum(marked, axis=2) > 0
    target = routes.reshape(micros, tokens * choices)
    if use_permutes(experts):
        target = target ^ my_index
    slot_of = jnp.where(present, target * capacity + position, -1)
    slot_of = jnp.transpose(slot_of.reshape(micros, tokens, choices), (0, 2, 1))
    slots = lax.broadcasted_iota(jnp.int32, (1, 1, experts * capacity, 1), 2)
    return (chosen, (slot_of[:, :, None, :] == slots).astype(BF16))


def local(inputs, cotangent, lengths, norm_gain, router, expert_in, expert_out, routes):
    micros, tokens, width = inputs.shape
    sections = lax.axis_size("section")
    section = lax.axis_index("section")
    router_local = router[0]
    experts = router_local.shape[1]
    choices = routes.shape[3]
    capacity = choices * tokens // experts
    gain_row = norm_gain[0]
    weight_in, weight_out = (expert_in[0, 0], expert_out[0, 0])
    last = sections - 1
    ticks = 2 * sections
    assert micros == 2 and choices == 2 and sections >= 3
    positions = lax.broadcasted_iota(jnp.int32, (micros, tokens), 1)
    chosen, tables = pair_tables(
        routes[0], positions < lengths, experts, capacity, lax.axis_index("expert")
    )
    is_last = section == last

    def first_at(tick):
        return tick if tick <= last else 2 * last - tick

    def pick(tick, pair):
        if tick == 0:
            return pair[0]
        if tick == ticks - 1:
            return pair[1]
        return jnp.where(section == first_at(tick), pair[0], pair[1])

    def kept(tick, store):
        early, late = (2 * last - tick, 2 * last + 2 - tick)
        if early not in store or late not in store:
            return store[early] if early in store else store[late]
        return jnp.where(section == early, store[early], store[late])

    hiddens, mixes, rows_home, weights_at, cot_rows = ({}, {}, {}, {}, {})
    inbox = None
    grads = [None, None]
    router_total = jnp.zeros((experts, width), F32)
    gain_total = jnp.zeros((width,), F32)
    for tick in range(ticks):
        forward = tick <= sections
        backward = tick >= last
        both = forward and backward
        table = pick(tick, tables)
        chosen_now = pick(tick, chosen)
        slot_table = jnp.sum(table, axis=0)
        if forward:
            hidden = inbox
            if tick < micros:
                hidden = inputs[tick] if tick == 0 else jnp.where(section == 0, inputs[tick], inbox)
            values, scale_inv, normed = normalize(hidden, gain_row)
            hiddens[tick] = hidden
            source = normed
            if tick < micros:
                source = jnp.where(is_last, cotangent[tick], normed)
        if backward:
            grad = inbox
            if both:
                grad = jnp.where(is_last, cotangent[tick - last], inbox)
            if tick > last:
                source = jnp.where(is_last, normed, grad) if both else grad
        outgoing = dot(slot_table, source).astype(BF16)
        received = exchange(outgoing, experts)
        if tick < micros:
            cot_rows[tick] = received

        if forward:
            logits = dot(normed, router_local)
            picked = jnp.sum(jnp.where(chosen_now, logits[:, None, :], 0.0), axis=-1)
            weights_at[tick] = jax.nn.sigmoid(picked - picked[:, ::-1])

        if not backward:
            mixes[tick] = dot(received, weight_in)
            result = dot(activate(mixes[tick]), weight_out).astype(BF16)
        elif tick == last:

            def visit_once(packed):
                rows, grad_rows = packed
                mixed = dot(rows, weight_in)
                back, choice_grad = adjoint(mixed, grad_rows, weight_in, weight_out)
                return (back, split_pair(choice_grad), mixed)

            def visit_forward(packed):
                mixed = dot(packed[0], weight_in)
                out = dot(activate(mixed), weight_out).astype(BF16)
                return (out, jnp.zeros((out.shape[0], EXTRA), BF16), mixed)

            result, extra, mixes[tick] = lax.cond(
                is_last, visit_once, visit_forward, (received, cot_rows[0])
            )
            result = jnp.concatenate([result, extra], axis=1)
        elif both:
            mixed = lax.cond(
                is_last, lambda rows: dot(rows, weight_in), lambda rows: mixes[last - 1], received
            )
            grad_rows = jnp.where(is_last, cot_rows[1], received)
            result, choice_grad = adjoint(mixed, grad_rows, weight_in, weight_out)
            result = jnp.concatenate([result, split_pair(choice_grad)], axis=1)
        else:
            result = adjoint(kept(tick, mixes), received, weight_in, weight_out)[0]
        returned = exchange(result, experts)
        per_choice = jnp.einsum("kst,sd->ktd", table, returned, preferred_element_type=F32)
        extra_back = per_choice[:, :, width:]
        per_choice = per_choice[:, :, :width]

        if forward:
            rows_home[tick] = returned[:, :width]
            weights = jnp.transpose(weights_at[tick])[:, :, None]
            leaving = (values + jnp.sum(weights * per_choice, axis=0)).astype(BF16)
        if backward:
            values, scale_inv, normed = normalize(kept(tick, hiddens), gain_row)
            weights = kept(tick, weights_at)
            grad_values = grad.astype(F32)
            if both:
                choice_grad = extra_back[:, :, 0] + extra_back[:, :, 1]
            if tick > last:
                outputs = kept(tick, {k: v for k, v in rows_home.items() if k < sections})
                outputs = jnp.einsum("kst,sd->ktd", table, outputs, preferred_element_type=F32)
                stored_grad = jnp.sum(grad_values[None] * outputs, axis=-1)
                choice_grad = jnp.where(is_last, choice_grad, stored_grad) if both else stored_grad
            first_grad = weights[:, 0] * weights[:, 1] * (choice_grad[0] - choice_grad[1])
            pick_grad = jnp.stack([first_grad, -first_grad], axis=1)
            logit_grad = jnp.sum(jnp.where(chosen_now, pick_grad[:, :, None], 0.0), axis=1)
            logit_grad = logit_grad.astype(BF16)
            normed_grad = jnp.sum(jnp.transpose(weights)[:, :, None] * per_choice, axis=0)
            normed_grad = normed_grad + dot_t(logit_grad, router_local)
            centred = values * scale_inv
            scaled_grad = normed_grad * gain_row
            input_grad = grad_values + scale_inv * (
                scaled_grad - centred * jnp.mean(scaled_grad * centred, axis=-1, keepdims=True)
            )
            input_grad = input_grad.astype(BF16)
            active = (section == 2 * last - tick) | (section == 2 * last + 1 - tick)
            router_piece = lax.dot_general(
                logit_grad, normed, (((0,), (0,)), ((), ())), preferred_element_type=F32
            )
            router_total = router_total + jnp.where(active, router_piece, 0.0)
            gain_total = gain_total + jnp.where(active, jnp.sum(normed_grad * centred, axis=0), 0.0)
            leaving = jnp.where(is_last, input_grad, leaving) if tick == last else input_grad
            for micro in range(micros):
                here = section == 2 * last + micro - tick
                if grads[micro] is None:
                    grads[micro] = input_grad
                else:
                    grads[micro] = jnp.where(here, input_grad, grads[micro])
        if tick < ticks - 1:
            route = []
            for micro in range(micros):
                step = tick - micro
                if 0 <= step < 2 * last:
                    route.append((first_at(step), first_at(step + 1)))
            inbox = lax.ppermute(leaving, "section", route)
    router_sum = lax.psum(router_total, "expert")
    gain_sum = lax.psum(gain_total, "expert")
    denominator = micros * choices * tokens
    return (
        jnp.stack(grads)[None],
        jnp.transpose(router_sum / denominator)[None],
        (gain_sum / denominator)[None],
    )


def solution(mesh):
    in_specs = (
        P(None, "expert", None),
        P(None, "expert", None),
        P(None, "expert"),
        P("section", None),
        P("section", None, None),
        P("section", "expert", None, None),
        P("section", "expert", None, None),
        P("section", None, "expert", None),
    )
    out_specs = (P("section", None, "expert", None), P("section", None, None), P("section", None))
    return jax.shard_map(local, mesh=mesh, in_specs=in_specs, out_specs=out_specs, check_vma=False)
```

```python
import jax
import jax.numpy as jnp
from jax import lax
from jax.experimental import pallas as pl
from jax.experimental.pallas import tpu as pltpu
from jax.sharding import PartitionSpec as P

EPSILON = 1e-06
EXTRA = 128
MIB = 1 << 20
LIMIT_EXPERT = 10
LIMIT_HOME = 10
F32 = jnp.float32
BF16 = jnp.bfloat16
VMEM = pltpu.MemorySpace.VMEM
SMEM = pltpu.MemorySpace.SMEM


def scale_of(values):
    return lax.rsqrt(jnp.mean(values * values, axis=-1, keepdims=True) + EPSILON)


def dot(a, b):
    return jnp.dot(a, b, preferred_element_type=F32)


def dot_t(a, b):
    return lax.dot_general(a, b, (((1,), (1,)), ((), ())), preferred_element_type=F32)


def dot_first(a, b):
    return lax.dot_general(a, b, (((0,), (0,)), ((), ())), preferred_element_type=F32)


def power_of_two(count):
    return count & (count - 1) == 0


def use_permutes(count):
    return 2 <= count <= 8 and power_of_two(count)


def hop(block, sections, experts, flip):
    route = [
        (j * experts + e, sections[j] * experts + (e ^ flip))
        for j in range(len(sections))
        for e in range(experts)
    ]
    return lax.ppermute(block, ("section", "expert"), route)


def parts_of(experts, size):
    half = experts * size // 2
    return [(0, half), (half, half)] if use_permutes(experts) else [(0, 2 * half)]


def places_of(experts, size):
    if not use_permutes(experts):
        return [[(0, 0, experts * size)]]
    half = experts * size // 2
    return [[(0, z * size, size), (size, half + z * size, size)] for z in range(experts // 2)]


def exchange(parts, sections, experts):
    rows, width = parts[0].shape
    stay = list(range(len(sections)))
    if not use_permutes(experts):
        shape = (experts, rows // experts, width)
        block = lax.all_to_all(parts[0].reshape(shape), "expert", 0, 0, tiled=True)
        block = block.reshape(rows, width)
        return [block if sections == stay else hop(block, sections, experts, 0)]
    size = 2 * rows // experts
    near, far = parts
    far = hop(far, stay, experts, 1)
    got = []
    for z in reversed(range(experts // 2)):
        span = slice(z * size, (z + 1) * size)
        message = jnp.concatenate([near[span], far[span]], axis=0)
        moves = z > 0 or sections != stay
        got.insert(0, hop(message, sections, experts, 2 * z) if moves else message)
    return got


def total(value, experts):
    if not use_permutes(experts):
        return lax.psum(value, "expert")

    def moved(flip):
        return lax.ppermute(value, "expert", [(i, i ^ flip) for i in range(experts)])

    value = value + moved(1)
    terms = [value] + [moved(flip) for flip in range(2, experts, 2)]
    while len(terms) > 1:
        terms = [terms[i] + terms[i + 1] for i in range(0, len(terms), 2)]
    return terms[0]


def slots_of(routes, length, my_index, experts, capacity):
    tokens = routes.shape[0]
    live = lax.broadcasted_iota(jnp.int32, (tokens, 1), 0) < length
    codes = lax.broadcasted_iota(jnp.int32, (tokens, experts), 1)
    marked = [
        jnp.where((routes[:, k : k + 1] == codes) & live, 1.0, 0.0).astype(F32) for k in range(2)
    ]
    below = lax.broadcasted_iota(jnp.int32, (tokens, tokens), 1)
    below = below < lax.broadcasted_iota(jnp.int32, (tokens, tokens), 0)
    below = jnp.where(below, 1.0, 0.0).astype(BF16)
    earlier = dot(below, (marked[0] + marked[1]).astype(BF16))
    columns = []
    for k in range(2):
        position = jnp.sum(earlier * marked[k], axis=1, keepdims=True).astype(jnp.int32)
        target = routes[:, k : k + 1]
        if use_permutes(experts):
            flips = target ^ my_index
            target = (flips & 1) * (experts // 2) + (flips >> 1)
        columns.append(jnp.where(live, target * capacity + position, -1))
    return columns


def one_hot(column, slots):
    codes = lax.broadcasted_iota(jnp.int32, (column.shape[0], slots), 1)
    return jnp.where(column == codes, 1.0, 0.0).astype(BF16)


def gathered(columns, source, parts, outs, slots):
    table = one_hot(columns[0], slots) + one_hot(columns[1], slots)
    for out, (start, count) in zip(outs, parts):
        out[...] = dot_first(table[:, start : start + count], source).astype(BF16)


def load_rows(refs, places, rows):
    for ref, place in zip(refs, places):
        for source, slot, size in place:
            rows[slot : slot + size, :] = ref[source : source + size, :]


def last_section():
    return lax.axis_index("section") == lax.axis_size("section") - 1


def first_at(tick, sections):
    return tick if tick < sections else 2 * sections - 2 - tick


def micro_at(tick, section, sections):
    if tick == 0 or tick == 2 * sections - 1:
        return 0 if tick == 0 else 1
    return jnp.where(section == first_at(tick, sections), 0, 1)


def goes_to(order, section):
    if order == [j ^ 1 for j in range(len(order))]:
        return section ^ 1
    return lax.rem(section + order[0], len(order))


def first_step(lengths, inputs, cotangent, routes, experts, slots):
    _, tokens, width = inputs.shape
    parts = parts_of(experts, slots // experts)

    def kernel(lengths_ref, inputs_ref, cot_ref, routes_ref, *outs):
        my_index = lax.axis_index("expert")
        columns = slots_of(routes_ref[0], lengths_ref[0, 0], my_index, experts, slots // experts)
        source = jnp.where(last_section(), cot_ref[0], inputs_ref[0])
        gathered(columns, source, parts, outs, slots)

    block = pl.BlockSpec((1, tokens, width), lambda i: (0, 0, 0))
    return list(
        pl.pallas_call(
            kernel,
            grid=(1,),
            out_shape=[jax.ShapeDtypeStruct((n, width), BF16) for _, n in parts],
            in_specs=[
                pl.BlockSpec(memory_space=SMEM),
                block,
                block,
                pl.BlockSpec((1,) + routes.shape[1:], lambda i: (0, 0, 0)),
            ],
            out_specs=[pl.BlockSpec((n, width), lambda i: (0, 0)) for _, n in parts],
            compiler_params=pltpu.CompilerParams(vmem_limit_bytes=LIMIT_HOME * MIB),
        )(lengths, inputs, cotangent, routes)
    )


def slots_step(lengths, all_routes, experts, slots):
    micros = lengths.shape[0]

    def kernel(lengths_ref, *refs):
        my_index = lax.axis_index("expert")
        for routes_ref, out in zip(refs, refs[len(all_routes) :]):
            for m in range(micros):
                columns = slots_of(
                    routes_ref[m], lengths_ref[m, 0], my_index, experts, slots // experts
                )
                out[m, :, 0:1] = columns[0]
                out[m, :, 1:2] = columns[1]

    outputs = [(routes.shape, jnp.int32) for routes in all_routes]
    return call(kernel, [lengths] + all_routes, {0}, outputs, [], LIMIT_HOME * MIB, 1 << 16, 1 << 16)


def router_step(routes, grad, difference, weights, hidden, gain, experts):
    width = hidden.shape[1]

    def kernel(routes_ref, grad_ref, difference_ref, weights_ref, hidden_ref, gain_ref, out):
        values = hidden_ref[...].astype(F32)
        normed = (values * scale_of(values) * gain_ref[...]).astype(BF16)
        grads = grad_ref[...].astype(F32)
        change = jnp.sum(grads * difference_ref[...], axis=1, keepdims=True)
        first_grad = weights_ref[:, 0:1] * weights_ref[:, 1:2] * change
        out[...] = dot_first(logit_grads(routes_ref[1], first_grad, experts), normed)

    inputs = [routes, grad, difference, weights, hidden, gain]
    outputs = [((experts, width), F32)]
    return call(kernel, inputs, set(), outputs, [], LIMIT_HOME * MIB, 1 << 20, 1 << 20)[0]


def logit_grads(routes, first_grad, experts):
    codes = lax.broadcasted_iota(jnp.int32, (routes.shape[0], experts), 1)
    own = jnp.where(routes[:, 0:1] == codes, first_grad, 0.0)
    return (own - jnp.where(routes[:, 1:2] == codes, first_grad, 0.0)).astype(BF16)


def call(kernel, inputs, in_smem, outputs, scratch, limit, flops, moved):
    specs = [pl.BlockSpec(memory_space=SMEM if i in in_smem else VMEM) for i in range(len(inputs))]
    return pl.pallas_call(
        kernel,
        out_shape=[jax.ShapeDtypeStruct(s, d) for s, d in outputs],
        in_specs=specs,
        out_specs=[pl.BlockSpec(memory_space=VMEM)] * len(outputs),
        scratch_shapes=scratch,
        compiler_params=pltpu.CompilerParams(vmem_limit_bytes=limit),
        cost_estimate=pl.CostEstimate(flops=flops, bytes_accessed=moved, transcendentals=0),
    )(*inputs)


def expert_step(kind, messages, cots, mixed, gain, weight_in, weight_out, experts, slots):
    width, hidden = (weight_in.shape[0], weight_out.shape[0])
    tile = 256 if hidden % 256 == 0 else hidden
    wide = 512 if width % 512 == 0 else width
    size = slots // experts
    places, parts = (places_of(experts, size), parts_of(experts, size))
    extra = EXTRA if kind in ("turn", "fold") else 0
    names = []
    inputs = []

    def add(name, value):
        names.append(name)
        inputs.append(value)

    for i, message in enumerate(messages):
        add(("message", i), message)
    if extra:
        for i, message in enumerate(cots):
            add(("cot", i), message)
    if kind in ("fold", "backward"):
        add("mixed", mixed)
    if kind != "backward":
        add("gain", gain)
    add("in", weight_in)
    add("out", weight_out)
    outputs = [((n, width + extra), BF16) for _, n in parts]
    keeps = kind in ("forward", "turn")
    if keeps:
        outputs.append(((slots, 2 * hidden), F32))

    def kernel(*refs):
        ref = dict(zip(names, refs[: len(names)]))
        outs = refs[len(names) : len(names) + len(outputs)]
        rows, grads, joined, pair = refs[len(names) + len(outputs) :]
        message_refs = [ref["message", i] for i in range(len(messages))]
        w_in, w_out = (ref["in"], ref["out"])

        def normed_rows():
            load_rows(message_refs, places, rows)
            values = rows[...].astype(F32)
            rows[...] = (values * scale_of(values) * ref["gain"][...]).astype(BF16)

        def spans(f):
            return (slice(f * tile, (f + 1) * tile), slice(hidden + f * tile, hidden + (f + 1) * tile))

        def mix(f):
            gate, up = spans(f)
            return (dot(rows[...], w_in[:, gate]), dot(rows[...], w_in[:, up]))

        def finish(product):
            for n in range(width // wide):
                span = slice(n * wide, (n + 1) * wide)
                rows_out = product(span)
                for out, (start, count) in zip(outs, parts):
                    out[:, span] = rows_out[start : start + count].astype(BF16)

        def forward():
            normed_rows()
            for f in range(hidden // tile):
                gate, up = spans(f)
                g, u = mix(f)
                if keeps:
                    outs[-1][:, gate] = g
                    outs[-1][:, up] = u
                joined[:, gate] = (g * jax.nn.sigmoid(g) * u).astype(BF16)
            finish(lambda span: dot(joined[:, :hidden], w_out[:, span]))

        def adjoint(f, g, u):
            gate, up = spans(f)
            act_grad = dot_t(grads[...], w_out[gate, :])
            s = jax.nn.sigmoid(g)
            joined[:, gate] = (act_grad * u * s * (1.0 + g * (1.0 - s))).astype(BF16)
            joined[:, up] = (act_grad * g * s).astype(BF16)
            if extra:
                pair[...] += jnp.sum(act_grad * (g * s * u), axis=1, keepdims=True)

        def visit():
            normed_rows()
            load_rows([ref["cot", i] for i in range(len(cots))], places, grads)
            pair[...] = jnp.zeros_like(pair)
            for f in range(hidden // tile):
                adjoint(f, *mix(f))
            finish(lambda span: dot_t(joined[...], w_in[span, :]))

        def backward():
            load_rows(message_refs, places, grads)
            if extra:
                pair[...] = jnp.zeros_like(pair)
            for f in range(hidden // tile):
                gate, up = spans(f)
                adjoint(f, ref["mixed"][:, gate], ref["mixed"][:, up])
            finish(lambda span: dot_t(joined[...], w_in[span, :]))

        if kind == "forward":
            forward()
        elif kind == "backward":
            backward()
        else:
            pl.when(last_section())(visit)
            pl.when(jnp.logical_not(last_section()))(forward if kind == "turn" else backward)
        for out, (start, count) in zip(outs, parts):
            if extra:
                value = pair[start : start + count, :]
                high = value.astype(BF16).astype(F32)
                lane = lax.broadcasted_iota(jnp.int32, (count, extra), 1)
                low = jnp.where(lane == 1, value - high, 0.0)
                out[:, width:] = jnp.where(lane == 0, high, low).astype(BF16)

    scratch = [
        pltpu.VMEM((slots, width), BF16),
        pltpu.VMEM((slots, width), BF16),
        pltpu.VMEM((slots, 2 * hidden), BF16),
        pltpu.VMEM((slots, 1), F32),
    ]
    flops = 2 * slots * width * hidden * (6 if extra else 3)
    found = call(kernel, inputs, set(), outputs, scratch, LIMIT_EXPERT * MIB, flops, 6 * width * hidden)
    return (found[: len(parts)], found[-1] if keeps else None)


def home_step(kind, tick, returned, routes, slot_own, slot_next, order, alt, forward, backward, experts, slots):
    names, inputs = ([], [])

    def add(name, value):
        names.append(name)
        inputs.append(value)

    for i, message in enumerate(returned):
        add(("message", i), message)
    add("routes", routes)
    add("slot", slot_own)
    if slot_next is not None:
        add("next", slot_next)
    if alt is not None:
        add("alt_inputs", alt[0])
        add("alt_cot", alt[1])
    if forward is not None:
        for name, value in forward.items():
            add(name, value)
    if backward is not None:
        for name, value in backward.items():
            add(name, value)
    wide = returned[0].shape[1]
    tokens, width = (forward or backward)["hidden"].shape
    size = slots // experts
    places, parts = (places_of(experts, size), parts_of(experts, size))
    out_names, outputs = ([], [])

    def give(name, shape, kind_of):
        out_names.append(name)
        outputs.append((shape, kind_of))

    give("leaving", (tokens, width), BF16)
    if slot_next is not None:
        for i, (_, n) in enumerate(parts):
            give(("part", i), (n, width), BF16)
    if forward is not None:
        give("weights", (tokens, 2), F32)
        give("difference", (tokens, width), F32)
    if backward is not None:
        give("gain_piece", (1, width), F32)
        if slot_next is not None:
            give("router_piece", (experts, width), F32)

    def kernel(*refs):
        ref = dict(zip(names, refs[: len(names)]))
        out = dict(zip(out_names, refs[len(names) : len(names) + len(outputs)]))
        (rows,) = refs[len(names) + len(outputs) :]
        load_rows([ref["message", i] for i in range(len(returned))], places, rows)
        values = ref["hidden"][...].astype(F32)
        scale = scale_of(values)
        normed = (values * scale * ref["gain"][...]).astype(BF16)
        section = lax.axis_index("section")
        sections = lax.axis_size("section")
        micro = micro_at(tick, section, sections)
        routes_now = ref["routes"][micro]
        slot_now = ref["slot"][micro]
        expert_codes = lax.broadcasted_iota(jnp.int32, (tokens, experts), 1)
        chosen = [routes_now[:, k : k + 1] == expert_codes for k in range(2)]

        def picked(k):
            return dot(one_hot(slot_now[:, k : k + 1], slots), rows[...])

        def weigh():
            logits = dot(normed, ref["router"][...])
            first, second = [
                jnp.sum(jnp.where(c, logits, 0.0), axis=1, keepdims=True) for c in chosen
            ]
            return (jax.nn.sigmoid(first - second), jax.nn.sigmoid(second - first))

        def run_forward():
            first, second = (picked(0)[:, :width], picked(1)[:, :width])
            w0, w1 = weigh()
            out["weights"][:, 0:1] = w0
            out["weights"][:, 1:2] = w1
            out["difference"][...] = first - second
            out["leaving"][...] = (values + (w0 * first + w1 * second)).astype(BF16)

        def run_backward(fresh):
            first, second = (picked(0), picked(1))
            if fresh is None or fresh:
                pair = first[:, width:] - second[:, width:]
                lane = lax.broadcasted_iota(jnp.int32, pair.shape, 1)
                change = jnp.sum(jnp.where(lane < 2, pair, 0.0), axis=1, keepdims=True)
            grad = ref["grad"][...].astype(F32)
            if fresh is None or not fresh:
                stored = jnp.sum(grad * ref["difference"][...], axis=1, keepdims=True)
                change = stored if fresh is not None else jnp.where(last_section(), change, stored)
            if "weights" in ref:
                w0, w1 = (ref["weights"][:, 0:1], ref["weights"][:, 1:2])
            else:
                w0, w1 = weigh()
            first_grad = w0 * w1 * change
            logit_grad = logit_grads(routes_now, first_grad, experts)
            normed_grad = w0 * first[:, :width] + w1 * second[:, :width]
            normed_grad += dot_t(logit_grad, ref["router"][...])
            centred = values * scale
            scaled = normed_grad * ref["gain"][...]
            mean = jnp.mean(scaled * centred, axis=-1, keepdims=True)
            out["leaving"][...] = (grad + scale * (scaled - centred * mean)).astype(BF16)
            out["gain_piece"][...] = jnp.sum(normed_grad * centred, axis=0, keepdims=True)
            if "router_piece" in out:
                out["router_piece"][...] = dot_first(logit_grad, normed)

        if kind == "forward":
            run_forward()
        elif kind == "backward":
            run_backward(False)
        elif kind == "fold":
            run_backward(None)
        else:
            pl.when(last_section())(lambda: run_backward(True))
            pl.when(jnp.logical_not(last_section()))(run_forward)
        if slot_next is not None:
            at = goes_to(order, section)
            columns = ref["next"][micro_at(tick + 1, at, sections)]
            columns = [columns[:, 0:1], columns[:, 1:2]]
            source = out["leaving"][...]
            if alt is not None:
                source = jnp.where(at == 0, ref["alt_inputs"][1], source)
                source = jnp.where(at == sections - 1, ref["alt_cot"][1], source)
            outs = [out["part", i] for i in range(len(parts))]
            gathered(columns, source, parts, outs, slots)

    scratch = [pltpu.VMEM((slots, wide), BF16)]
    moved = 16 * tokens * width
    flops = 2 * slots * tokens * width * 3
    found = call(kernel, inputs, set(), outputs, scratch, LIMIT_HOME * MIB, flops, moved)
    return dict(zip(out_names, found))


def local(inputs, cotangent, lengths, norm_gain, router, expert_in, expert_out, routes):
    micros, tokens, width = inputs.shape
    sections = lax.axis_size("section")
    section = lax.axis_index("section")
    router_local = router[0]
    experts = router_local.shape[1]
    choices = routes.shape[3]
    capacity = choices * tokens // experts
    slots = experts * capacity
    weight_in, weight_out = (expert_in[0, 0], expert_out[0, 0])
    last = sections - 1
    ticks = 2 * sections
    stay = list(range(sections))
    assert micros == 2 and choices == 2 and sections >= 3 and sections % 2 == 0
    is_last = section == last
    def sections_after(tick):
        active = []
        for micro in range(micros):
            step = tick - micro
            if 0 <= step < 2 * last:
                active.append((first_at(step, sections), first_at(step + 1, sections)))
        swap = [j ^ 1 for j in stay]
        up = [(j + 1) % sections for j in stay]
        down = [(j - 1) % sections for j in stay]
        for choice in (swap, up, down):
            if all(choice[a] == b for a, b in active):
                return choice
        raise ValueError("no route")

    def kept(tick, store):
        early, late = (2 * last - tick, 2 * last + 2 - tick)
        if early not in store or late not in store:
            return store[early] if early in store else store[late]
        return jnp.where(section == early, store[early], store[late])

    orders = {}
    for tick in range(ticks - 1):
        orders.setdefault(tuple(sections_after(tick)), None)
    gain = norm_gain
    weights_at, differences, hiddens, mixes, cots = ({}, {}, {}, {}, {})
    inbox = None
    grads = [None, None]
    router_total = jnp.zeros((experts, width), F32)
    gain_total = jnp.zeros((1, width), F32)
    sent = first_step(lengths, inputs, cotangent, routes[0], experts, slots)
    received = exchange(sent, stay, experts)
    mine, first = lax.optimization_barrier((routes[0], received[-1]))
    received = received[:-1] + [first]
    for order in orders:
        back = [order.index(j) for j in stay]
        orders[order] = hop(mine, back, experts, 0)
    slot_own, *found = slots_step(lengths, [routes[0]] + list(orders.values()), experts, slots)
    orders = dict(zip(orders, found))
    for tick in range(ticks):
        forward = tick <= last
        backward = tick >= last
        kind = "forward" if tick < last else "turn" if tick == last else "backward"
        kind = "fold" if tick == sections else kind
        if tick < micros:
            cots[tick] = received
        mixed = None
        if tick == sections:
            mixed = mixes[last - 1]
        elif tick > sections:
            mixed = kept(tick, mixes)
        cot = cots[tick - last] if kind in ("turn", "fold") else None
        result, mixes[tick] = expert_step(
            kind, received, cot, mixed, gain, weight_in, weight_out, experts, slots
        )
        returned = exchange(result, stay, experts)
        if tick > 0:
            inbox, first = lax.optimization_barrier((inbox, returned[-1]))
            returned = returned[:-1] + [first]

        hidden = inbox
        if tick < micros:
            hidden = inputs[tick] if tick == 0 else jnp.where(section == 0, inputs[tick], inbox)
        common = {"gain": gain, "router": router_local}
        ahead, behind = (None, None)
        if tick <= sections:
            hiddens[tick] = hidden
        if forward:
            ahead = {"hidden": hidden, **common}
        if backward:
            grad = inbox
            if tick <= sections:
                grad = jnp.where(is_last, cotangent[tick - last], inbox)
            behind = {"grad": grad}
            if tick > last:
                behind["hidden"] = kept(tick, hiddens)
                behind["difference"] = kept(tick, differences)
                if tick > sections:
                    behind["weights"] = kept(tick, weights_at)
                behind.update(common)
        slot_next, alt, sections_to = (None, None, None)
        if tick < ticks - 1:
            sections_to = sections_after(tick)
            slot_next = orders[tuple(sections_to)]
        else:
            piece = router_step(
                routes[0], grad, behind["difference"], behind["weights"], behind["hidden"], gain, experts
            )
            router_total = router_total + jnp.where(section == 0, piece, 0.0)
            router_sum = total(router_total, experts) / (micros * choices * tokens)
        if tick == 0:
            alt = (inputs, cotangent)
        found = home_step(
            kind, tick, returned, routes[0], slot_own, slot_next, sections_to, alt, ahead, behind, experts, slots
        )
        leaving = found["leaving"]
        if forward:
            weights_at[tick] = found["weights"]
            differences[tick] = found["difference"]
        if backward:
            active = (section == 2 * last - tick) | (section == 2 * last + 1 - tick)
            if tick < ticks - 1:
                router_total = router_total + jnp.where(active, found["router_piece"], 0.0)
            gain_total = gain_total + jnp.where(active, found["gain_piece"], 0.0)
            for micro in range(micros):
                here = section == 2 * last + micro - tick
                if grads[micro] is None:
                    grads[micro] = leaving
                else:
                    grads[micro] = jnp.where(here, leaving, grads[micro])
        if tick < ticks - 1:
            sent = [found["part", i] for i in range(len(sent))]
            received = exchange(sent, sections_to, experts)
            leaving, first = lax.optimization_barrier((leaving, received[-1]))
            received = received[:-1] + [first]
            inbox = hop(leaving, sections_to, experts, 0)
    gain_sum = total(gain_total, experts) / (micros * choices * tokens)
    return (jnp.stack(grads)[None], jnp.transpose(router_sum)[None], gain_sum)


def solution(mesh):
    in_specs = (
        P(None, "expert", None),
        P(None, "expert", None),
        P(None, "expert"),
        P("section", None),
        P("section", None, None),
        P("section", "expert", None, None),
        P("section", "expert", None, None),
        P("section", None, "expert", None),
    )
    out_specs = (P("section", None, "expert", None), P("section", None, None), P("section", None))
    return jax.shard_map(local, mesh=mesh, in_specs=in_specs, out_specs=out_specs, check_vma=False)
```

```python
import jax
import jax.numpy as jnp
from jax import lax
from jax.experimental import pallas as pl
from jax.experimental.pallas import tpu as pltpu
from jax.sharding import PartitionSpec as P

EPSILON = 1e-06
EXTRA = 128
MIB = 1 << 20
PACK = 256
DIRECT_BACK = False
LIMIT_EXPERT = 10
LIMIT_HOME = 10
F32 = jnp.float32
BF16 = jnp.bfloat16
VMEM = pltpu.MemorySpace.VMEM
SMEM = pltpu.MemorySpace.SMEM
HBM = pltpu.MemorySpace.HBM


def scale_of(values):
    return lax.rsqrt(jnp.mean(values * values, axis=-1, keepdims=True) + EPSILON)


def dot(a, b):
    return jnp.dot(a, b, preferred_element_type=F32)


def dot_t(a, b):
    return lax.dot_general(a, b, (((1,), (1,)), ((), ())), preferred_element_type=F32)


def dot_first(a, b):
    return lax.dot_general(a, b, (((0,), (0,)), ((), ())), preferred_element_type=F32)


def power_of_two(count):
    return count & (count - 1) == 0


def use_permutes(count):
    return 2 <= count <= 8 and power_of_two(count)


def hop(block, sections, experts, flip):
    route = [
        (j * experts + e, sections[j] * experts + (e ^ flip))
        for j in range(len(sections))
        for e in range(experts)
    ]
    return lax.ppermute(block, ("section", "expert"), route)


def block_at(flip, experts):
    return (flip & 1) * (experts // 2) + (flip >> 1)


def parts_of(experts, size, direct=False):
    if not use_permutes(experts):
        return [(0, experts * size)]
    if direct:
        return [(block_at(flip, experts) * size, size) for flip in range(experts)]
    half = experts * size // 2
    return [(0, half), (half, half)]


def places_of(experts, size, direct=False):
    if not use_permutes(experts):
        return [[(0, 0, experts * size)]]
    if direct:
        return [[(0, start, count)] for start, count in parts_of(experts, size, True)]
    half = experts * size // 2
    return [[(0, z * size, size), (size, half + z * size, size)] for z in range(experts // 2)]


def pack_step(near, far, size):
    rows, width = near.shape
    count = rows // size

    def kernel(near_ref, far_ref, *outs):
        for z, out in enumerate(outs):
            out[:size, :] = near_ref[z * size : (z + 1) * size, :]
            out[size:, :] = far_ref[z * size : (z + 1) * size, :]

    return pl.pallas_call(
        kernel,
        out_shape=[pltpu.VMEM((2 * size, width), near.dtype)] * count,
        in_specs=[pl.BlockSpec(memory_space=VMEM)] * 2,
        out_specs=[pl.BlockSpec(memory_space=VMEM)] * count,
        compiler_params=pltpu.CompilerParams(vmem_limit_bytes=LIMIT_HOME * MIB),
    )(near, far)


def exchange(parts, sections, experts, direct=False, packed=False):
    rows, width = parts[0].shape
    stay = list(range(len(sections)))
    if not use_permutes(experts):
        shape = (experts, rows // experts, width)
        block = lax.all_to_all(parts[0].reshape(shape), "expert", 0, 0, tiled=True)
        block = block.reshape(rows, width)
        return [block if sections == stay else hop(block, sections, experts, 0)]
    if direct:
        far = [hop(parts[x], sections, experts, x) for x in reversed(range(1, experts))]
        return [parts[0]] + far[::-1]
    size = 2 * rows // experts
    near, far = parts
    far = hop(far, stay, experts, 1)
    got = []
    messages = pack_step(near, far, size) if packed else None
    for z in reversed(range(experts // 2)):
        span = slice(z * size, (z + 1) * size)
        message = messages[z] if packed else jnp.concatenate([near[span], far[span]], axis=0)
        moves = z > 0 or sections != stay
        got.insert(0, hop(message, sections, experts, 2 * z) if moves else message)
    return got


def total(value, experts):
    if not use_permutes(experts):
        return lax.psum(value, "expert")

    def moved(flip):
        return lax.ppermute(value, "expert", [(i, i ^ flip) for i in range(experts)])

    value = value + moved(1)
    terms = [value] + [moved(flip) for flip in range(2, experts, 2)]
    while len(terms) > 1:
        terms = [terms[i] + terms[i + 1] for i in range(0, len(terms), 2)]
    return terms[0]


def slots_of(routes, length, my_index, experts, capacity):
    tokens = routes.shape[0]
    live = lax.broadcasted_iota(jnp.int32, (tokens, 1), 0) < length
    codes = lax.broadcasted_iota(jnp.int32, (tokens, experts), 1)
    marked = [
        jnp.where((routes[:, k : k + 1] == codes) & live, 1.0, 0.0).astype(F32) for k in range(2)
    ]
    below = lax.broadcasted_iota(jnp.int32, (tokens, tokens), 1)
    below = below < lax.broadcasted_iota(jnp.int32, (tokens, tokens), 0)
    below = jnp.where(below, 1.0, 0.0).astype(BF16)
    earlier = dot(below, (marked[0] + marked[1]).astype(BF16))
    columns = []
    for k in range(2):
        position = jnp.sum(earlier * marked[k], axis=1, keepdims=True).astype(jnp.int32)
        target = routes[:, k : k + 1]
        if use_permutes(experts):
            flips = target ^ my_index
            target = block_at(flips, experts)
        columns.append(jnp.where(live, target * capacity + position, -1))
    return columns


def one_hot(column, slots):
    codes = lax.broadcasted_iota(jnp.int32, (column.shape[0], slots), 1)
    return jnp.where(column == codes, 1.0, 0.0).astype(BF16)


def gathered(columns, source, parts, outs, slots):
    table = one_hot(columns[0], slots) + one_hot(columns[1], slots)
    for out, (start, count) in zip(outs, parts):
        out[...] = dot_first(table[:, start : start + count], source).astype(BF16)


def load_rows(refs, places, rows):
    for ref, place in zip(refs, places):
        for source, slot, size in place:
            rows[slot : slot + size, :] = ref[source : source + size, :]


def last_section():
    return lax.axis_index("section") == lax.axis_size("section") - 1


def first_at(tick, sections):
    return tick if tick < sections else 2 * sections - 2 - tick


def micro_at(tick, section, sections):
    if tick == 0 or tick == 2 * sections - 1:
        return 0 if tick == 0 else 1
    return jnp.where(section == first_at(tick, sections), 0, 1)


def goes_to(order, section):
    if order == [j ^ 1 for j in range(len(order))]:
        return section ^ 1
    return lax.rem(section + order[0], len(order))


def first_step(lengths, inputs, cotangent, routes, experts, slots):
    _, tokens, width = inputs.shape
    capacity = slots // experts
    parts = parts_of(experts, capacity)

    def kernel(lengths_ref, inputs_ref, cot_ref, routes_ref, *refs):
        outs, source, arrived = (refs[: len(parts)], refs[-2], refs[-1])
        here = last_section()

        @pl.when(here)
        def _():
            pltpu.make_async_copy(cot_ref.at[0], source, arrived).start()

        @pl.when(jnp.logical_not(here))
        def _():
            pltpu.make_async_copy(inputs_ref.at[0], source, arrived).start()

        my_index = lax.axis_index("expert")
        live = lax.broadcasted_iota(jnp.int32, (1, tokens), 1) < lengths_ref[0, 0]
        codes = lax.broadcasted_iota(jnp.int32, (experts, tokens), 0)
        rows = [routes_ref[0, k : k + 1, :] for k in range(2)]
        marked = [jnp.where((row == codes) & live, 1.0, 0.0).astype(F32) for row in rows]
        above = lax.broadcasted_iota(jnp.int32, (tokens, tokens), 0)
        above = above < lax.broadcasted_iota(jnp.int32, (tokens, tokens), 1)
        above = jnp.where(above, 1.0, 0.0).astype(BF16)
        earlier = dot((marked[0] + marked[1]).astype(BF16), above)
        slot_codes = lax.broadcasted_iota(jnp.int32, (slots, tokens), 0)
        table = jnp.zeros((slots, tokens), BF16)
        for k in range(2):
            position = jnp.sum(earlier * marked[k], axis=0, keepdims=True).astype(jnp.int32)
            target = rows[k]
            if use_permutes(experts):
                target = block_at(target ^ my_index, experts)
            slot = jnp.where(live, target * capacity + position, -1)
            table += jnp.where(slot_codes == slot, 1.0, 0.0).astype(BF16)
        pltpu.make_async_copy(inputs_ref.at[0], source, arrived).wait()
        for out, (start, count) in zip(outs, parts):
            out[...] = dot(table[start : start + count], source[...]).astype(BF16)

    specs = [pl.BlockSpec(memory_space=kind) for kind in (SMEM, HBM, HBM, VMEM)]
    return list(
        pl.pallas_call(
            kernel,
            out_shape=[jax.ShapeDtypeStruct((n, width), BF16) for _, n in parts],
            in_specs=specs,
            out_specs=[pl.BlockSpec(memory_space=VMEM)] * len(parts),
            scratch_shapes=[pltpu.VMEM((tokens, width), BF16), pltpu.SemaphoreType.DMA(())],
            compiler_params=pltpu.CompilerParams(vmem_limit_bytes=LIMIT_HOME * MIB),
        )(lengths, *[pltpu.with_memory_space_constraint(x, HBM) for x in (inputs, cotangent)], routes)
    )


def load_step(weights):
    def kernel(*refs):
        count = len(weights)
        copies = [
            pltpu.make_async_copy(refs[i], refs[count + i], refs[-1].at[i]) for i in range(count)
        ]
        for copy in copies:
            copy.start()
        for copy in copies:
            copy.wait()

    return pl.pallas_call(
        kernel,
        out_shape=[pltpu.VMEM(w.shape, w.dtype) for w in weights],
        in_specs=[pl.BlockSpec(memory_space=HBM)] * len(weights),
        out_specs=[pl.BlockSpec(memory_space=VMEM)] * len(weights),
        scratch_shapes=[pltpu.SemaphoreType.DMA((len(weights),))],
        compiler_params=pltpu.CompilerParams(vmem_limit_bytes=LIMIT_HOME * MIB),
    )(*[pltpu.with_memory_space_constraint(w, HBM) for w in weights])


def slots_step(lengths, all_routes, experts, slots):
    micros = lengths.shape[1]

    def kernel(lengths_ref, *refs):
        my_index = lax.axis_index("expert")
        for routes_ref, out in zip(refs, refs[len(all_routes) :]):
            for m in range(micros):
                columns = slots_of(
                    routes_ref[m], lengths_ref[0, m], my_index, experts, slots // experts
                )
                out[m, :, 0:1] = columns[0]
                out[m, :, 1:2] = columns[1]

    outputs = [(routes.shape, jnp.int32) for routes in all_routes]
    return call(kernel, [lengths] + all_routes, {0}, outputs, [], LIMIT_HOME * MIB, 1 << 16, 1 << 16)


def logit_grads(routes, first_grad, experts):
    codes = lax.broadcasted_iota(jnp.int32, (routes.shape[0], experts), 1)
    own = jnp.where(routes[:, 0:1] == codes, first_grad, 0.0)
    return (own - jnp.where(routes[:, 1:2] == codes, first_grad, 0.0)).astype(BF16)


def call(kernel, inputs, in_smem, outputs, scratch, limit, flops, moved, in_hbm=()):
    kinds = [SMEM if i in in_smem else HBM if i in in_hbm else VMEM for i in range(len(inputs))]
    specs = [pl.BlockSpec(memory_space=kind) for kind in kinds]
    return pl.pallas_call(
        kernel,
        out_shape=[jax.ShapeDtypeStruct(s, d) for s, d in outputs],
        in_specs=specs,
        out_specs=[pl.BlockSpec(memory_space=VMEM)] * len(outputs),
        scratch_shapes=scratch,
        compiler_params=pltpu.CompilerParams(vmem_limit_bytes=limit),
        cost_estimate=pl.CostEstimate(flops=flops, bytes_accessed=moved, transcendentals=0),
    )(*inputs)


def expert_step(kind, messages, cots, mixed, gain, weight_in, weight_out, experts, slots):
    width, hidden = (weight_in.shape[0], weight_out.shape[0])
    tile = 256 if hidden % 256 == 0 else hidden
    wide = 512 if width % 512 == 0 else width
    size = slots // experts
    places, parts = (places_of(experts, size), parts_of(experts, size, DIRECT_BACK))
    extra = EXTRA if kind in ("turn", "fold") else 0
    names = []
    inputs = []

    def add(name, value):
        names.append(name)
        inputs.append(value)

    for i, message in enumerate(messages):
        add(("message", i), message)
    if extra:
        for i, message in enumerate(cots):
            add(("cot", i), message)
    if kind in ("fold", "backward"):
        add("mixed", mixed)
    if kind != "backward":
        add("gain", gain)
    add("in", pltpu.with_memory_space_constraint(weight_in, VMEM))
    add("out", pltpu.with_memory_space_constraint(weight_out, VMEM))
    outputs = [((n, width + extra), BF16) for _, n in parts]
    keeps = kind in ("forward", "turn")
    if keeps:
        outputs.append(((slots, 2 * hidden), F32))

    def kernel(*refs):
        ref = dict(zip(names, refs[: len(names)]))
        outs = refs[len(names) : len(names) + len(outputs)]
        rows, grads, joined, pair = refs[len(names) + len(outputs) :]
        message_refs = [ref["message", i] for i in range(len(messages))]
        w_in, w_out = (ref["in"], ref["out"])

        def normed_rows():
            load_rows(message_refs, places, rows)
            values = rows[...].astype(F32)
            rows[...] = (values * scale_of(values) * ref["gain"][...]).astype(BF16)

        def spans(f):
            return (slice(f * tile, (f + 1) * tile), slice(hidden + f * tile, hidden + (f + 1) * tile))

        def mix(f):
            gate, up = spans(f)
            return (dot(rows[...], w_in[:, gate]), dot(rows[...], w_in[:, up]))

        def finish(product):
            for n in range(width // wide):
                span = slice(n * wide, (n + 1) * wide)
                rows_out = product(span)
                for out, (start, count) in zip(outs, parts):
                    out[:, span] = rows_out[start : start + count].astype(BF16)

        def forward():
            normed_rows()
            for f in range(hidden // tile):
                gate, up = spans(f)
                g, u = mix(f)
                if keeps:
                    outs[-1][:, gate] = g
                    outs[-1][:, up] = u
                joined[:, gate] = (g * jax.nn.sigmoid(g) * u).astype(BF16)
            finish(lambda span: dot(joined[:, :hidden], w_out[:, span]))

        def adjoint(f, g, u):
            gate, up = spans(f)
            act_grad = dot_t(grads[...], w_out[gate, :])
            s = jax.nn.sigmoid(g)
            joined[:, gate] = (act_grad * u * s * (1.0 + g * (1.0 - s))).astype(BF16)
            joined[:, up] = (act_grad * g * s).astype(BF16)
            if extra:
                pair[...] += jnp.sum(act_grad * (g * s * u), axis=1, keepdims=True)

        def visit():
            normed_rows()
            load_rows([ref["cot", i] for i in range(len(cots))], places, grads)
            pair[...] = jnp.zeros_like(pair)
            for f in range(hidden // tile):
                adjoint(f, *mix(f))
            finish(lambda span: dot_t(joined[...], w_in[span, :]))

        def backward():
            load_rows(message_refs, places, grads)
            if extra:
                pair[...] = jnp.zeros_like(pair)
            for f in range(hidden // tile):
                gate, up = spans(f)
                adjoint(f, ref["mixed"][:, gate], ref["mixed"][:, up])
            finish(lambda span: dot_t(joined[...], w_in[span, :]))

        if kind == "forward":
            forward()
        elif kind == "backward":
            backward()
        else:
            pl.when(last_section())(visit)
            pl.when(jnp.logical_not(last_section()))(forward if kind == "turn" else backward)
        for out, (start, count) in zip(outs, parts):
            if extra:
                value = pair[start : start + count, :]
                high = value.astype(BF16).astype(F32)
                lane = lax.broadcasted_iota(jnp.int32, (count, extra), 1)
                low = jnp.where(lane == 1, value - high, 0.0)
                out[:, width:] = jnp.where(lane == 0, high, low).astype(BF16)

    scratch = [
        pltpu.VMEM((slots, width), BF16),
        pltpu.VMEM((slots, width), BF16),
        pltpu.VMEM((slots, 2 * hidden), BF16),
        pltpu.VMEM((slots, 1), F32),
    ]
    flops = 2 * slots * width * hidden * (6 if extra else 3)
    found = call(kernel, inputs, set(), outputs, scratch, LIMIT_EXPERT * MIB, flops, 6 * width * hidden)
    return (found[: len(parts)], found[-1] if keeps else None)


def home_step(kind, tick, returned, routes, slot_own, slot_next, order, alt, forward, backward, experts, slots):
    names, inputs, in_hbm = ([], [], set())

    def add(name, value):
        names.append(name)
        inputs.append(value)

    for i, message in enumerate(returned):
        add(("message", i), message)
    add("routes", routes)
    add("slot", slot_own)
    if slot_next is not None:
        add("next", slot_next)
    if alt is not None:
        in_hbm.update((len(names), len(names) + 1))
        add("alt_inputs", pltpu.with_memory_space_constraint(alt[0], HBM))
        add("alt_cot", pltpu.with_memory_space_constraint(alt[1], HBM))
    if forward is not None:
        for name, value in forward.items():
            add(name, value)
    if backward is not None:
        for name, value in backward.items():
            add(name, value)
    wide = returned[0].shape[1]
    tokens, width = (forward or backward)["hidden"].shape
    size = slots // experts
    places, parts = (places_of(experts, size, DIRECT_BACK), parts_of(experts, size))
    out_names, outputs = ([], [])

    def give(name, shape, kind_of):
        out_names.append(name)
        outputs.append((shape, kind_of))

    give("leaving", (tokens, width), BF16)
    if slot_next is not None:
        for i, (_, n) in enumerate(parts):
            give(("part", i), (n, width), BF16)
    if forward is not None:
        give("weights", (tokens, 2), F32)
        give("difference", (tokens, width), F32)
    if backward is not None:
        if slot_next is not None:
            give("sums", (experts + 8, width), F32)
        else:
            give("packed", ((experts + 1) * (width // PACK), PACK), F32)

    def kernel(*refs):
        ref = dict(zip(names, refs[: len(names)]))
        out = dict(zip(out_names, refs[len(names) : len(names) + len(outputs)]))
        rows, *held = refs[len(names) + len(outputs) :]
        section = lax.axis_index("section")
        sections = lax.axis_size("section")
        if alt is not None:
            held, arrived = held
            at = goes_to(order, section)
            from_inputs = pltpu.make_async_copy(ref["alt_inputs"].at[1], held, arrived)
            from_cot = pltpu.make_async_copy(ref["alt_cot"].at[1], held, arrived)
            pl.when(at == sections - 1)(from_cot.start)
            pl.when(at != sections - 1)(from_inputs.start)
        load_rows([ref["message", i] for i in range(len(returned))], places, rows)
        values = ref["hidden"][...].astype(F32)
        scale = scale_of(values)
        normed = (values * scale * ref["gain"][...]).astype(BF16)
        micro = micro_at(tick, section, sections)
        routes_now = ref["routes"][micro]
        slot_now = ref["slot"][micro]
        expert_codes = lax.broadcasted_iota(jnp.int32, (tokens, experts), 1)
        chosen = [routes_now[:, k : k + 1] == expert_codes for k in range(2)]

        def picked(k):
            return dot(one_hot(slot_now[:, k : k + 1], slots), rows[...])

        def weigh():
            logits = dot_t(normed, ref["router"][...])
            first, second = [
                jnp.sum(jnp.where(c, logits, 0.0), axis=1, keepdims=True) for c in chosen
            ]
            return (jax.nn.sigmoid(first - second), jax.nn.sigmoid(second - first))

        def run_forward():
            first, second = (picked(0)[:, :width], picked(1)[:, :width])
            w0, w1 = weigh()
            out["weights"][:, 0:1] = w0
            out["weights"][:, 1:2] = w1
            out["difference"][...] = first - second
            out["leaving"][...] = (values + (w0 * first + w1 * second)).astype(BF16)

        def run_backward(fresh):
            first, second = (picked(0), picked(1))
            if fresh is None or fresh:
                pair = first[:, width:] - second[:, width:]
                lane = lax.broadcasted_iota(jnp.int32, pair.shape, 1)
                change = jnp.sum(jnp.where(lane < 2, pair, 0.0), axis=1, keepdims=True)
            grad = ref["grad"][...].astype(F32)
            if fresh is None or not fresh:
                stored = jnp.sum(grad * ref["difference"][...], axis=1, keepdims=True)
                change = stored if fresh is not None else jnp.where(last_section(), change, stored)
            if "weights" in ref:
                w0, w1 = (ref["weights"][:, 0:1], ref["weights"][:, 1:2])
            else:
                w0, w1 = weigh()
            first_grad = w0 * w1 * change
            logit_grad = logit_grads(routes_now, first_grad, experts)
            normed_grad = w0 * first[:, :width] + w1 * second[:, :width]
            normed_grad += dot(logit_grad, ref["router"][...])
            centred = values * scale
            scaled = normed_grad * ref["gain"][...]
            mean = jnp.mean(scaled * centred, axis=-1, keepdims=True)
            out["leaving"][...] = (grad + scale * (scaled - centred * mean)).astype(BF16)
            active = (section == 2 * sections - 2 - tick) | (section == 2 * sections - 1 - tick)
            piece = dot_first(logit_grad, normed)
            gains = jnp.sum(normed_grad * centred, axis=0, keepdims=True)
            before = ref["sums"][...] if "sums" in ref else jnp.zeros((experts + 8, width), F32)
            piece = before[:experts] + jnp.where(active, piece, 0.0)
            gains = before[experts:] + jnp.where(active, gains, 0.0)
            if "sums" in out:
                out["sums"][:experts, :] = piece
                out["sums"][experts:, :] = gains
                return
            count = width // PACK
            for row in range(experts + 1):
                value = piece[row : row + 1] if row < experts else gains[:1]
                for q in range(count):
                    at = row * count + q
                    out["packed"][at : at + 1, :] = value[:, q * PACK : (q + 1) * PACK]

        if kind == "forward":
            run_forward()
        elif kind == "backward":
            run_backward(False)
        elif kind == "fold":
            run_backward(None)
        else:
            pl.when(last_section())(lambda: run_backward(True))
            @pl.when(jnp.logical_not(last_section()))
            def _():
                out["sums"][...] = jnp.zeros_like(out["sums"])
                run_forward()

        if slot_next is not None:
            at = goes_to(order, section)
            columns = ref["next"][micro_at(tick + 1, at, sections)]
            columns = [columns[:, 0:1], columns[:, 1:2]]
            source = out["leaving"][...]
            if alt is not None:
                from_inputs.wait()
                source = jnp.where((at == 0) | (at == sections - 1), held[...], source)
            outs = [out["part", i] for i in range(len(parts))]
            gathered(columns, source, parts, outs, slots)

    scratch = [pltpu.VMEM((slots, wide), BF16)]
    if alt is not None:
        scratch += [pltpu.VMEM((tokens, width), BF16), pltpu.SemaphoreType.DMA(())]
    moved = 16 * tokens * width
    flops = 2 * slots * tokens * width * 3
    found = call(kernel, inputs, set(), outputs, scratch, LIMIT_HOME * MIB, flops, moved, in_hbm)
    return dict(zip(out_names, found))


def local(inputs, cotangent, lengths, norm_gain, router, expert_in, expert_out, routes):
    micros, tokens, width = inputs.shape
    sections = lax.axis_size("section")
    section = lax.axis_index("section")
    router_local = jnp.transpose(router[0])
    experts = router_local.shape[0]
    choices = routes.shape[3]
    capacity = choices * tokens // experts
    slots = experts * capacity
    weight_in, weight_out = (expert_in[0, 0], expert_out[0, 0])
    last = sections - 1
    ticks = 2 * sections
    stay = list(range(sections))
    assert micros == 2 and choices == 2 and sections >= 3 and sections % 2 == 0
    is_last = section == last
    def sections_after(tick):
        active = []
        for micro in range(micros):
            step = tick - micro
            if 0 <= step < 2 * last:
                active.append((first_at(step, sections), first_at(step + 1, sections)))
        swap = [j ^ 1 for j in stay]
        up = [(j + 1) % sections for j in stay]
        down = [(j - 1) % sections for j in stay]
        for choice in (swap, up, down):
            if all(choice[a] == b for a, b in active):
                return choice
        raise ValueError("no route")

    def kept(tick, store):
        early, late = (2 * last - tick, 2 * last + 2 - tick)
        if early not in store or late not in store:
            return store[early] if early in store else store[late]
        return jnp.where(section == early, store[early], store[late])

    orders = {}
    for tick in range(ticks - 1):
        orders.setdefault(tuple(sections_after(tick)), None)
    gain = norm_gain
    weights_at, differences, hiddens, mixes, cots = ({}, {}, {}, {}, {})
    inbox = None
    grads = [None, None]
    sums = None
    lengths = jnp.transpose(lengths)
    by_choice = jnp.swapaxes(routes[0], -1, -2)
    sent = first_step(lengths, inputs, cotangent, by_choice, experts, slots)
    received = exchange(sent, stay, experts)
    mine, in_first, out_first, first = lax.optimization_barrier(
        (routes[0], weight_in, weight_out, received[0])
    )
    received = [first] + received[1:]
    in_first, weight_out = load_step([in_first, out_first])
    for order in orders:
        back = [order.index(j) for j in stay]
        orders[order] = hop(mine, back, experts, 0)
    slot_own, *found = slots_step(lengths, [routes[0]] + list(orders.values()), experts, slots)
    orders = dict(zip(orders, found))
    for tick in range(ticks):
        forward = tick <= last
        backward = tick >= last
        kind = "forward" if tick < last else "turn" if tick == last else "backward"
        kind = "fold" if tick == sections else kind
        if tick < micros:
            cots[tick] = received
        mixed = None
        if tick == sections:
            mixed = mixes[last - 1]
        elif tick > sections:
            mixed = kept(tick, mixes)
        cot = cots[tick - last] if kind in ("turn", "fold") else None
        in_now = in_first if tick == 0 else weight_in
        if tick in (1, 2, ticks - 1):
            in_now, first = lax.optimization_barrier((weight_in, received[-1]))
            received = received[:-1] + [first]
            (in_now,) = load_step([in_now])
        result, mixes[tick] = expert_step(
            kind, received, cot, mixed, gain, in_now, weight_out, experts, slots
        )
        returned = exchange(result, stay, experts, DIRECT_BACK)
        if tick > 0:
            inbox, first = lax.optimization_barrier((inbox, returned[-1]))
            returned = returned[:-1] + [first]

        hidden = inbox
        if tick < micros:
            hidden = inputs[tick] if tick == 0 else jnp.where(section == 0, inputs[tick], inbox)
        common = {"gain": gain, "router": router_local}
        ahead, behind = (None, None)
        if tick <= sections:
            hiddens[tick] = hidden
        if forward:
            ahead = {"hidden": hidden, **common}
        if backward:
            grad = inbox
            if tick <= sections:
                grad = jnp.where(is_last, cotangent[tick - last], inbox)
            behind = {"grad": grad}
            if sums is not None:
                behind["sums"] = sums
            if tick > last:
                behind["hidden"] = kept(tick, hiddens)
                behind["difference"] = kept(tick, differences)
                if tick > sections:
                    behind["weights"] = kept(tick, weights_at)
                behind.update(common)
        slot_next, alt, sections_to = (None, None, None)
        if tick < ticks - 1:
            sections_to = sections_after(tick)
            slot_next = orders[tuple(sections_to)]
        if tick == 0:
            alt = (inputs, cotangent)
        found = home_step(
            kind, tick, returned, routes[0], slot_own, slot_next, sections_to, alt, ahead, behind, experts, slots
        )
        leaving = found["leaving"]
        if forward:
            weights_at[tick] = found["weights"]
            differences[tick] = found["difference"]
        if backward:
            sums = found["sums" if tick < ticks - 1 else "packed"]
            for micro in range(micros):
                here = section == 2 * last + micro - tick
                if grads[micro] is None:
                    grads[micro] = leaving
                else:
                    grads[micro] = jnp.where(here, leaving, grads[micro])
        if tick < ticks - 1:
            sent = [found["part", i] for i in range(len(sent))]
            received = exchange(sent, sections_to, experts, packed=tick in (0, 1, ticks - 2))
            leaving, first = lax.optimization_barrier((leaving, received[-1]))
            received = received[:-1] + [first]
            inbox = hop(leaving, sections_to, experts, 0)
    sums = total(sums, experts) / (micros * choices * tokens)
    sums = sums.reshape(experts + 1, width)
    router_sum = jnp.transpose(sums[:experts])
    return (jnp.stack(grads)[None], router_sum[None], sums[experts : experts + 1])


def solution(mesh):
    in_specs = (
        P(None, "expert", None),
        P(None, "expert", None),
        P(None, "expert"),
        P("section", None),
        P("section", None, None),
        P("section", "expert", None, None),
        P("section", "expert", None, None),
        P("section", None, "expert", None),
    )
    out_specs = (P("section", None, "expert", None), P("section", None, None), P("section", None))
    return jax.shard_map(local, mesh=mesh, in_specs=in_specs, out_specs=out_specs, check_vma=False)
```

```python
import jax
import jax.numpy as jnp
from jax import lax
from jax.experimental import pallas as pl
from jax.experimental.pallas import tpu as pltpu
from jax.sharding import PartitionSpec as P

EPSILON = 1e-06
EXTRA = 128
MIB = 1 << 20
PACK = 256
DIRECT_BACK = False
LIMIT_EXPERT = 10
LIMIT_HOME = 10
F32 = jnp.float32
BF16 = jnp.bfloat16
VMEM = pltpu.MemorySpace.VMEM
SMEM = pltpu.MemorySpace.SMEM
HBM = pltpu.MemorySpace.HBM


def scale_of(values):
    return lax.rsqrt(jnp.mean(values * values, axis=-1, keepdims=True) + EPSILON)


def dot(a, b):
    return jnp.dot(a, b, preferred_element_type=F32)


def dot_t(a, b):
    return lax.dot_general(a, b, (((1,), (1,)), ((), ())), preferred_element_type=F32)


def dot_first(a, b):
    return lax.dot_general(a, b, (((0,), (0,)), ((), ())), preferred_element_type=F32)


def power_of_two(count):
    return count & (count - 1) == 0


def use_permutes(count):
    return 2 <= count <= 8 and power_of_two(count)


def hop(block, sections, experts, flip):
    route = [
        (j * experts + e, sections[j] * experts + (e ^ flip))
        for j in range(len(sections))
        for e in range(experts)
    ]
    return lax.ppermute(block, ("section", "expert"), route)


def block_at(flip, experts):
    return (flip & 1) * (experts // 2) + (flip >> 1)


def parts_of(experts, size, direct=False):
    if not use_permutes(experts):
        return [(0, experts * size)]
    if direct:
        return [(block_at(flip, experts) * size, size) for flip in range(experts)]
    half = experts * size // 2
    return [(0, half), (half, half)]


def places_of(experts, size, direct=False):
    if not use_permutes(experts):
        return [[(0, 0, experts * size)]]
    if direct:
        return [[(0, start, count)] for start, count in parts_of(experts, size, True)]
    half = experts * size // 2
    return [[(0, z * size, size), (size, half + z * size, size)] for z in range(experts // 2)]


def pack_step(near, far, size):
    rows, width = near.shape
    count = rows // size

    def kernel(near_ref, far_ref, *outs):
        for z, out in enumerate(outs):
            out[:size, :] = near_ref[z * size : (z + 1) * size, :]
            out[size:, :] = far_ref[z * size : (z + 1) * size, :]

    return pl.pallas_call(
        kernel,
        out_shape=[pltpu.VMEM((2 * size, width), near.dtype)] * count,
        in_specs=[pl.BlockSpec(memory_space=VMEM)] * 2,
        out_specs=[pl.BlockSpec(memory_space=VMEM)] * count,
        compiler_params=pltpu.CompilerParams(vmem_limit_bytes=LIMIT_HOME * MIB),
    )(near, far)


def exchange(parts, sections, experts, direct=False, packed=False):
    rows, width = parts[0].shape
    stay = list(range(len(sections)))
    if not use_permutes(experts):
        shape = (experts, rows // experts, width)
        block = lax.all_to_all(parts[0].reshape(shape), "expert", 0, 0, tiled=True)
        block = block.reshape(rows, width)
        return [block if sections == stay else hop(block, sections, experts, 0)]
    if direct:
        far = [hop(parts[x], sections, experts, x) for x in reversed(range(1, experts))]
        return [parts[0]] + far[::-1]
    size = 2 * rows // experts
    near, far = parts
    far = hop(far, stay, experts, 1)
    got = []
    messages = pack_step(near, far, size) if packed else None
    for z in reversed(range(experts // 2)):
        span = slice(z * size, (z + 1) * size)
        message = messages[z] if packed else jnp.concatenate([near[span], far[span]], axis=0)
        moves = z > 0 or sections != stay
        got.insert(0, hop(message, sections, experts, 2 * z) if moves else message)
    return got


def total(value, experts):
    if not use_permutes(experts):
        return lax.psum(value, "expert")

    def moved(flip):
        return lax.ppermute(value, "expert", [(i, i ^ flip) for i in range(experts)])

    value = value + moved(1)
    terms = [value] + [moved(flip) for flip in range(2, experts, 2)]
    while len(terms) > 1:
        terms = [terms[i] + terms[i + 1] for i in range(0, len(terms), 2)]
    return terms[0]


def slots_of(routes, length, my_index, experts, capacity):
    tokens = routes.shape[0]
    live = lax.broadcasted_iota(jnp.int32, (tokens, 1), 0) < length
    codes = lax.broadcasted_iota(jnp.int32, (tokens, experts), 1)
    marked = [
        jnp.where((routes[:, k : k + 1] == codes) & live, 1.0, 0.0).astype(F32) for k in range(2)
    ]
    below = lax.broadcasted_iota(jnp.int32, (tokens, tokens), 1)
    below = below < lax.broadcasted_iota(jnp.int32, (tokens, tokens), 0)
    below = jnp.where(below, 1.0, 0.0).astype(BF16)
    earlier = dot(below, (marked[0] + marked[1]).astype(BF16))
    columns = []
    for k in range(2):
        position = jnp.sum(earlier * marked[k], axis=1, keepdims=True).astype(jnp.int32)
        target = routes[:, k : k + 1]
        if use_permutes(experts):
            flips = target ^ my_index
            target = block_at(flips, experts)
        columns.append(jnp.where(live, target * capacity + position, -1))
    return columns


def one_hot(column, slots):
    codes = lax.broadcasted_iota(jnp.int32, (column.shape[0], slots), 1)
    return jnp.where(column == codes, 1.0, 0.0).astype(BF16)


def gathered(columns, source, parts, outs, slots):
    table = one_hot(columns[0], slots) + one_hot(columns[1], slots)
    for out, (start, count) in zip(outs, parts):
        out[...] = dot_first(table[:, start : start + count], source).astype(BF16)


def load_rows(refs, places, rows):
    for ref, place in zip(refs, places):
        for source, slot, size in place:
            rows[slot : slot + size, :] = ref[source : source + size, :]


def last_section():
    return lax.axis_index("section") == lax.axis_size("section") - 1


def first_at(tick, sections):
    return tick if tick < sections else 2 * sections - 2 - tick


def micro_at(tick, section, sections):
    if tick == 0 or tick == 2 * sections - 1:
        return 0 if tick == 0 else 1
    return jnp.where(section == first_at(tick, sections), 0, 1)


def goes_to(order, section):
    if order == [j ^ 1 for j in range(len(order))]:
        return section ^ 1
    return lax.rem(section + order[0], len(order))


def first_step(lengths, inputs, cotangent, routes, experts, slots):
    _, tokens, width = inputs.shape
    capacity = slots // experts
    parts = parts_of(experts, capacity)

    def kernel(lengths_ref, inputs_ref, cot_ref, routes_ref, *refs):
        outs, source, arrived = (refs[: len(parts)], refs[-2], refs[-1])
        here = last_section()

        @pl.when(here)
        def _():
            pltpu.make_async_copy(cot_ref.at[0], source, arrived).start()

        @pl.when(jnp.logical_not(here))
        def _():
            pltpu.make_async_copy(inputs_ref.at[0], source, arrived).start()

        my_index = lax.axis_index("expert")
        live = lax.broadcasted_iota(jnp.int32, (1, tokens), 1) < lengths_ref[0, 0]
        codes = lax.broadcasted_iota(jnp.int32, (experts, tokens), 0)
        rows = [routes_ref[0, k : k + 1, :] for k in range(2)]
        marked = [jnp.where((row == codes) & live, 1.0, 0.0).astype(F32) for row in rows]
        above = lax.broadcasted_iota(jnp.int32, (tokens, tokens), 0)
        above = above < lax.broadcasted_iota(jnp.int32, (tokens, tokens), 1)
        above = jnp.where(above, 1.0, 0.0).astype(BF16)
        earlier = dot((marked[0] + marked[1]).astype(BF16), above)
        slot_codes = lax.broadcasted_iota(jnp.int32, (slots, tokens), 0)
        table = jnp.zeros((slots, tokens), BF16)
        for k in range(2):
            position = jnp.sum(earlier * marked[k], axis=0, keepdims=True).astype(jnp.int32)
            target = rows[k]
            if use_permutes(experts):
                target = block_at(target ^ my_index, experts)
            slot = jnp.where(live, target * capacity + position, -1)
            table += jnp.where(slot_codes == slot, 1.0, 0.0).astype(BF16)
        pltpu.make_async_copy(inputs_ref.at[0], source, arrived).wait()
        for out, (start, count) in zip(outs, parts):
            out[...] = dot(table[start : start + count], source[...]).astype(BF16)

    specs = [pl.BlockSpec(memory_space=kind) for kind in (SMEM, HBM, HBM, VMEM)]
    return list(
        pl.pallas_call(
            kernel,
            out_shape=[jax.ShapeDtypeStruct((n, width), BF16) for _, n in parts],
            in_specs=specs,
            out_specs=[pl.BlockSpec(memory_space=VMEM)] * len(parts),
            scratch_shapes=[pltpu.VMEM((tokens, width), BF16), pltpu.SemaphoreType.DMA(())],
            compiler_params=pltpu.CompilerParams(vmem_limit_bytes=LIMIT_HOME * MIB),
        )(lengths, *[pltpu.with_memory_space_constraint(x, HBM) for x in (inputs, cotangent)], routes)
    )


def load_step(weights):
    def kernel(*refs):
        count = len(weights)
        copies = [
            pltpu.make_async_copy(refs[i], refs[count + i], refs[-1].at[i]) for i in range(count)
        ]
        for copy in copies:
            copy.start()
        for copy in copies:
            copy.wait()

    return pl.pallas_call(
        kernel,
        out_shape=[pltpu.VMEM(w.shape, w.dtype) for w in weights],
        in_specs=[pl.BlockSpec(memory_space=HBM)] * len(weights),
        out_specs=[pl.BlockSpec(memory_space=VMEM)] * len(weights),
        scratch_shapes=[pltpu.SemaphoreType.DMA((len(weights),))],
        compiler_params=pltpu.CompilerParams(vmem_limit_bytes=LIMIT_HOME * MIB),
    )(*[pltpu.with_memory_space_constraint(w, HBM) for w in weights])


def slots_step(lengths, all_routes, experts, slots):
    micros = lengths.shape[1]

    def kernel(lengths_ref, *refs):
        my_index = lax.axis_index("expert")
        outs = refs[len(all_routes) :]
        for routes_ref, out in zip(refs, outs):
            for m in range(micros):
                columns = slots_of(
                    routes_ref[m], lengths_ref[0, m], my_index, experts, slots // experts
                )
                out[m, :, 0:1] = columns[0]
                out[m, :, 1:2] = columns[1]
        even = lax.rem(lax.axis_index("section"), 2) == 0
        outs[3][...] = jnp.where(even, outs[1][...], outs[2][...])

    outputs = [(all_routes[0].shape, jnp.int32)] * 4
    return call(kernel, [lengths] + all_routes, {0}, outputs, [], LIMIT_HOME * MIB, 1 << 16, 1 << 16)


def logit_grads(routes, first_grad, experts):
    codes = lax.broadcasted_iota(jnp.int32, (routes.shape[0], experts), 1)
    own = jnp.where(routes[:, 0:1] == codes, first_grad, 0.0)
    return (own - jnp.where(routes[:, 1:2] == codes, first_grad, 0.0)).astype(BF16)


def call(kernel, inputs, in_smem, outputs, scratch, limit, flops, moved, in_hbm=()):
    kinds = [SMEM if i in in_smem else HBM if i in in_hbm else VMEM for i in range(len(inputs))]
    specs = [pl.BlockSpec(memory_space=kind) for kind in kinds]
    return pl.pallas_call(
        kernel,
        out_shape=[jax.ShapeDtypeStruct(s, d) for s, d in outputs],
        in_specs=specs,
        out_specs=[pl.BlockSpec(memory_space=VMEM)] * len(outputs),
        scratch_shapes=scratch,
        compiler_params=pltpu.CompilerParams(vmem_limit_bytes=limit),
        cost_estimate=pl.CostEstimate(flops=flops, bytes_accessed=moved, transcendentals=0),
    )(*inputs)


def expert_step(kind, messages, cot_act, mixed, gain, weight_in, weight_out, experts, slots):
    width, hidden = (weight_in.shape[0], weight_out.shape[0])
    tile = 256 if hidden % 256 == 0 else hidden
    wide = 512 if width % 512 == 0 else width
    size = slots // experts
    places, parts = (places_of(experts, size), parts_of(experts, size, DIRECT_BACK))
    extra = EXTRA if kind in ("turn", "fold") else 0
    names = []
    inputs = []

    def add(name, value):
        names.append(name)
        inputs.append(value)

    for i, message in enumerate(messages):
        add(("message", i), message)
    if extra:
        add("cot_act", cot_act)
    if kind in ("fold", "backward"):
        add("mixed", mixed)
    if kind != "backward":
        add("gain", gain)
    add("in", pltpu.with_memory_space_constraint(weight_in, VMEM))
    add("out", pltpu.with_memory_space_constraint(weight_out, VMEM))
    outputs = [((n, width + extra), BF16) for _, n in parts]
    keeps = kind in ("first", "forward", "turn")
    if keeps:
        outputs.append(((slots, 2 * hidden), F32))

    def kernel(*refs):
        ref = dict(zip(names, refs[: len(names)]))
        outs = refs[len(names) : len(names) + len(outputs)]
        rows, grads, joined, pair = refs[len(names) + len(outputs) :]
        message_refs = [ref["message", i] for i in range(len(messages))]
        w_in, w_out = (ref["in"], ref["out"])

        def normed_rows():
            load_rows(message_refs, places, rows)
            values = rows[...].astype(F32)
            rows[...] = (values * scale_of(values) * ref["gain"][...]).astype(BF16)

        def spans(f):
            return (slice(f * tile, (f + 1) * tile), slice(hidden + f * tile, hidden + (f + 1) * tile))

        def mix(f):
            gate, up = spans(f)
            return (dot(rows[...], w_in[:, gate]), dot(rows[...], w_in[:, up]))

        def finish(product):
            for n in range(width // wide):
                span = slice(n * wide, (n + 1) * wide)
                rows_out = product(span)
                for out, (start, count) in zip(outs, parts):
                    out[:, span] = rows_out[start : start + count].astype(BF16)

        def forward():
            normed_rows()
            for f in range(hidden // tile):
                gate, up = spans(f)
                g, u = mix(f)
                if keeps:
                    outs[-1][:, gate] = g
                    outs[-1][:, up] = u
                joined[:, gate] = (g * jax.nn.sigmoid(g) * u).astype(BF16)
            finish(lambda span: dot(joined[:, :hidden], w_out[:, span]))

        def cotangent():
            load_rows(message_refs, places, grads)
            for f in range(hidden // tile):
                gate, up = spans(f)
                outs[-1][:, gate] = dot_t(grads[...], w_out[gate, :])
                outs[-1][:, up] = jnp.zeros((slots, tile), F32)
            for out in outs[:-1]:
                out[...] = jnp.zeros_like(out)

        def adjoint(f, g, u, act_grad):
            gate, up = spans(f)
            s = jax.nn.sigmoid(g)
            joined[:, gate] = (act_grad * u * s * (1.0 + g * (1.0 - s))).astype(BF16)
            joined[:, up] = (act_grad * g * s).astype(BF16)
            if extra:
                pair[...] += jnp.sum(act_grad * (g * s * u), axis=1, keepdims=True)

        def visit():
            normed_rows()
            pair[...] = jnp.zeros_like(pair)
            for f in range(hidden // tile):
                adjoint(f, *mix(f), ref["cot_act"][:, spans(f)[0]])
            finish(lambda span: dot_t(joined[...], w_in[span, :]))

        def backward():
            load_rows(message_refs, places, grads)
            if extra:
                pair[...] = jnp.zeros_like(pair)
            for f in range(hidden // tile):
                gate, up = spans(f)
                act_grad = dot_t(grads[...], w_out[gate, :])
                adjoint(f, ref["mixed"][:, gate], ref["mixed"][:, up], act_grad)
            finish(lambda span: dot_t(joined[...], w_in[span, :]))

        if kind == "forward":
            forward()
        elif kind == "first":
            pl.when(last_section())(cotangent)
            pl.when(jnp.logical_not(last_section()))(forward)
        elif kind == "backward":
            backward()
        else:
            pl.when(last_section())(visit)
            pl.when(jnp.logical_not(last_section()))(forward if kind == "turn" else backward)
        for out, (start, count) in zip(outs, parts):
            if extra:
                value = pair[start : start + count, :]
                high = value.astype(BF16).astype(F32)
                lane = lax.broadcasted_iota(jnp.int32, (count, extra), 1)
                low = jnp.where(lane == 1, value - high, 0.0)
                out[:, width:] = jnp.where(lane == 0, high, low).astype(BF16)

    scratch = [
        pltpu.VMEM((slots, width), BF16),
        pltpu.VMEM((slots, width), BF16),
        pltpu.VMEM((slots, 2 * hidden), BF16),
        pltpu.VMEM((slots, 1), F32),
    ]
    flops = 2 * slots * width * hidden * (6 if extra else 3)
    found = call(kernel, inputs, set(), outputs, scratch, LIMIT_EXPERT * MIB, flops, 6 * width * hidden)
    return (found[: len(parts)], found[-1] if keeps else None)


def home_step(kind, tick, returned, routes, slot_own, slot_next, order, alt, forward, backward, experts, slots):
    names, inputs, in_hbm = ([], [], set())

    def add(name, value):
        names.append(name)
        inputs.append(value)

    for i, message in enumerate(returned):
        add(("message", i), message)
    add("routes", routes)
    add("slot", slot_own)
    if slot_next is not None:
        add("next", slot_next)
    if alt is not None:
        in_hbm.update((len(names), len(names) + 1))
        add("alt_inputs", pltpu.with_memory_space_constraint(alt[0], HBM))
        add("alt_cot", pltpu.with_memory_space_constraint(alt[1], HBM))
    if forward is not None:
        for name, value in forward.items():
            add(name, value)
    if backward is not None:
        for name, value in backward.items():
            add(name, value)
    wide = returned[0].shape[1]
    tokens, width = (forward or backward)["hidden"].shape
    size = slots // experts
    places, parts = (places_of(experts, size, DIRECT_BACK), parts_of(experts, size))
    out_names, outputs = ([], [])

    def give(name, shape, kind_of):
        out_names.append(name)
        outputs.append((shape, kind_of))

    give("leaving", (tokens, width), BF16)
    if slot_next is not None:
        for i, (_, n) in enumerate(parts):
            give(("part", i), (n, width), BF16)
    if forward is not None:
        give("weights", (tokens, 2), F32)
        give("difference", (tokens, width), F32)
    if backward is not None:
        if slot_next is not None:
            give("sums", (experts + 8, width), F32)
        else:
            give("packed", ((experts + 1) * (width // PACK), PACK), F32)

    def kernel(*refs):
        ref = dict(zip(names, refs[: len(names)]))
        out = dict(zip(out_names, refs[len(names) : len(names) + len(outputs)]))
        rows, *held = refs[len(names) + len(outputs) :]
        section = lax.axis_index("section")
        sections = lax.axis_size("section")
        if alt is not None:
            held, arrived = held
            at = goes_to(order, section)
            from_inputs = pltpu.make_async_copy(ref["alt_inputs"].at[1], held, arrived)
            from_cot = pltpu.make_async_copy(ref["alt_cot"].at[1], held, arrived)
            pl.when(at == sections - 1)(from_cot.start)
            pl.when(at != sections - 1)(from_inputs.start)
        load_rows([ref["message", i] for i in range(len(returned))], places, rows)
        values = ref["hidden"][...].astype(F32)
        scale = scale_of(values)
        normed = (values * scale * ref["gain"][...]).astype(BF16)
        micro = micro_at(tick, section, sections)
        routes_now = ref["routes"][micro]
        slot_now = ref["slot"][micro]
        expert_codes = lax.broadcasted_iota(jnp.int32, (tokens, experts), 1)
        chosen = [routes_now[:, k : k + 1] == expert_codes for k in range(2)]

        def picked(k):
            return dot(one_hot(slot_now[:, k : k + 1], slots), rows[...])

        def weigh():
            logits = dot_t(normed, ref["router"][...])
            first, second = [
                jnp.sum(jnp.where(c, logits, 0.0), axis=1, keepdims=True) for c in chosen
            ]
            return (jax.nn.sigmoid(first - second), jax.nn.sigmoid(second - first))

        def run_forward():
            first, second = (picked(0)[:, :width], picked(1)[:, :width])
            w0, w1 = weigh()
            out["weights"][:, 0:1] = w0
            out["weights"][:, 1:2] = w1
            out["difference"][...] = first - second
            out["leaving"][...] = (values + (w0 * first + w1 * second)).astype(BF16)

        def run_backward(fresh):
            first, second = (picked(0), picked(1))
            if fresh is None or fresh:
                pair = first[:, width:] - second[:, width:]
                lane = lax.broadcasted_iota(jnp.int32, pair.shape, 1)
                change = jnp.sum(jnp.where(lane < 2, pair, 0.0), axis=1, keepdims=True)
            grad = ref["grad"][...].astype(F32)
            if fresh is None or not fresh:
                stored = jnp.sum(grad * ref["difference"][...], axis=1, keepdims=True)
                change = stored if fresh is not None else jnp.where(last_section(), change, stored)
            if "weights" in ref:
                w0, w1 = (ref["weights"][:, 0:1], ref["weights"][:, 1:2])
            else:
                w0, w1 = weigh()
            first_grad = w0 * w1 * change
            logit_grad = logit_grads(routes_now, first_grad, experts)
            normed_grad = w0 * first[:, :width] + w1 * second[:, :width]
            normed_grad += dot(logit_grad, ref["router"][...])
            centred = values * scale
            scaled = normed_grad * ref["gain"][...]
            mean = jnp.mean(scaled * centred, axis=-1, keepdims=True)
            out["leaving"][...] = (grad + scale * (scaled - centred * mean)).astype(BF16)
            active = (section == 2 * sections - 2 - tick) | (section == 2 * sections - 1 - tick)
            piece = dot_first(logit_grad, normed)
            gains = jnp.sum(normed_grad * centred, axis=0, keepdims=True)
            before = ref["sums"][...] if "sums" in ref else jnp.zeros((experts + 8, width), F32)
            piece = before[:experts] + jnp.where(active, piece, 0.0)
            gains = before[experts:] + jnp.where(active, gains, 0.0)
            if "sums" in out:
                out["sums"][:experts, :] = piece
                out["sums"][experts:, :] = gains
                return
            count = width // PACK
            for row in range(experts + 1):
                value = piece[row : row + 1] if row < experts else gains[:1]
                for q in range(count):
                    at = row * count + q
                    out["packed"][at : at + 1, :] = value[:, q * PACK : (q + 1) * PACK]

        if kind == "forward":
            run_forward()
        elif kind == "backward":
            run_backward(False)
        elif kind == "fold":
            run_backward(None)
        else:
            pl.when(last_section())(lambda: run_backward(True))
            @pl.when(jnp.logical_not(last_section()))
            def _():
                out["sums"][...] = jnp.zeros_like(out["sums"])
                run_forward()

        if slot_next is not None:
            at = goes_to(order, section)
            columns = ref["next"][micro_at(tick + 1, at, sections)]
            columns = [columns[:, 0:1], columns[:, 1:2]]
            source = out["leaving"][...]
            if alt is not None:
                from_inputs.wait()
                source = jnp.where((at == 0) | (at == sections - 1), held[...], source)
            outs = [out["part", i] for i in range(len(parts))]
            gathered(columns, source, parts, outs, slots)

    scratch = [pltpu.VMEM((slots, wide), BF16)]
    if alt is not None:
        scratch += [pltpu.VMEM((tokens, width), BF16), pltpu.SemaphoreType.DMA(())]
    moved = 16 * tokens * width
    flops = 2 * slots * tokens * width * 3
    found = call(kernel, inputs, set(), outputs, scratch, LIMIT_HOME * MIB, flops, moved, in_hbm)
    return dict(zip(out_names, found))


def local(inputs, cotangent, lengths, norm_gain, router, expert_in, expert_out, routes):
    micros, tokens, width = inputs.shape
    sections = lax.axis_size("section")
    section = lax.axis_index("section")
    router_local = jnp.transpose(router[0])
    experts = router_local.shape[0]
    choices = routes.shape[3]
    capacity = choices * tokens // experts
    slots = experts * capacity
    weight_in, weight_out = (expert_in[0, 0], expert_out[0, 0])
    last = sections - 1
    ticks = 2 * sections
    stay = list(range(sections))
    assert micros == 2 and choices == 2 and sections >= 3 and sections % 2 == 0
    is_last = section == last
    def sections_after(tick):
        active = []
        for micro in range(micros):
            step = tick - micro
            if 0 <= step < 2 * last:
                active.append((first_at(step, sections), first_at(step + 1, sections)))
        swap = [j ^ 1 for j in stay]
        up = [(j + 1) % sections for j in stay]
        down = [(j - 1) % sections for j in stay]
        for choice in (swap, up, down):
            if all(choice[a] == b for a, b in active):
                return choice
        raise ValueError("no route")

    def kept(tick, store):
        early, late = (2 * last - tick, 2 * last + 2 - tick)
        if early not in store or late not in store:
            return store[early] if early in store else store[late]
        return jnp.where(section == early, store[early], store[late])

    gain = norm_gain
    weights_at, differences, hiddens, mixes = ({}, {}, {}, {})
    inbox = None
    grads = [None, None]
    sums = None
    lengths = jnp.transpose(lengths)
    by_choice = jnp.swapaxes(routes[0], -1, -2)
    sent = first_step(lengths, inputs, cotangent, by_choice, experts, slots)
    received = exchange(sent, stay, experts)
    mine, in_first, out_first, first = lax.optimization_barrier(
        (routes[0], weight_in, weight_out, received[0])
    )
    received = [first] + received[1:]
    in_first, weight_out = load_step([in_first, out_first])
    up, down = ([(j + d) % sections for j in stay] for d in (1, -1))
    known = [routes[0], hop(mine, down, experts, 0), hop(mine, up, experts, 0)]
    slot_own, slot_up, slot_down, slot_swap = slots_step(lengths, known, experts, slots)
    orders = {tuple(up): slot_up, tuple(down): slot_down, tuple(j ^ 1 for j in stay): slot_swap}
    for tick in range(ticks):
        forward = tick <= last
        backward = tick >= last
        kind = "forward" if tick < last else "turn" if tick == last else "backward"
        kind = "fold" if tick == sections else kind
        mixed = None
        if tick == sections:
            mixed = mixes[last - 1]
        elif tick > sections:
            mixed = kept(tick, mixes)
        cot = mixes[tick - last] if kind in ("turn", "fold") else None
        in_now = in_first if tick == 0 else weight_in
        if tick in (1, 2, ticks - 1):
            in_now, first = lax.optimization_barrier((weight_in, received[-1]))
            received = received[:-1] + [first]
            (in_now,) = load_step([in_now])
        result, mixes[tick] = expert_step(
            "first" if tick < micros else kind, received, cot, mixed, gain, in_now, weight_out, experts, slots
        )
        returned = exchange(result, stay, experts, DIRECT_BACK)
        if tick > 0:
            inbox, first = lax.optimization_barrier((inbox, returned[-1]))
            returned = returned[:-1] + [first]

        hidden = inbox
        if tick < micros:
            hidden = inputs[tick] if tick == 0 else jnp.where(section == 0, inputs[tick], inbox)
        common = {"gain": gain, "router": router_local}
        ahead, behind = (None, None)
        if tick <= sections:
            hiddens[tick] = hidden
        if forward:
            ahead = {"hidden": hidden, **common}
        if backward:
            grad = inbox
            if tick <= sections:
                grad = jnp.where(is_last, cotangent[tick - last], inbox)
            behind = {"grad": grad}
            if sums is not None:
                behind["sums"] = sums
            if tick > last:
                behind["hidden"] = kept(tick, hiddens)
                behind["difference"] = kept(tick, differences)
                if tick > sections:
                    behind["weights"] = kept(tick, weights_at)
                behind.update(common)
        slot_next, alt, sections_to = (None, None, None)
        if tick < ticks - 1:
            sections_to = sections_after(tick)
            slot_next = orders[tuple(sections_to)]
        if tick == 0:
            alt = (inputs, cotangent)
        found = home_step(
            kind, tick, returned, routes[0], slot_own, slot_next, sections_to, alt, ahead, behind, experts, slots
        )
        leaving = found["leaving"]
        if forward:
            weights_at[tick] = found["weights"]
            differences[tick] = found["difference"]
        if backward:
            sums = found["sums" if tick < ticks - 1 else "packed"]
            for micro in range(micros):
                here = section == 2 * last + micro - tick
                if grads[micro] is None:
                    grads[micro] = leaving
                else:
                    grads[micro] = jnp.where(here, leaving, grads[micro])
        if tick < ticks - 1:
            sent = [found["part", i] for i in range(len(sent))]
            received = exchange(sent, sections_to, experts, packed=tick in (0, 1, ticks - 2))
            leaving, first = lax.optimization_barrier((leaving, received[-1]))
            received = received[:-1] + [first]
            inbox = hop(leaving, sections_to, experts, 0)
    sums = total(sums, experts) / (micros * choices * tokens)
    sums = sums.reshape(experts + 1, width)
    router_sum = jnp.transpose(sums[:experts])
    return (jnp.stack(grads)[None], router_sum[None], sums[experts : experts + 1])


def solution(mesh):
    in_specs = (
        P(None, "expert", None),
        P(None, "expert", None),
        P(None, "expert"),
        P("section", None),
        P("section", None, None),
        P("section", "expert", None, None),
        P("section", "expert", None, None),
        P("section", None, "expert", None),
    )
    out_specs = (P("section", None, "expert", None), P("section", None, None), P("section", None))
    return jax.shard_map(local, mesh=mesh, in_specs=in_specs, out_specs=out_specs, check_vma=False)
```
